128 devices in a mesh: dp: 16 (over x, z_lo, core), col: 8 (over z_hi, y).
Axes of the slice: x: 4, y: 4, z: 4 (z_hi: 2, z_lo: 2; z = z_hi * 2 + z_lo), core: 2. Of those that a mesh axis runs over, the one named last changes fastest.
Arguments:
- tokens: bfloat16 [2048, 8192], P('col', 'dp'), may hold values from -6 to 6
- gate_weight: bfloat16 [8192, 14336], P('dp', 'col'), may hold values from -0.0625 to 0.0625
- up_weight: bfloat16 [8192, 14336], P('dp', 'col'), may hold values from -0.0625 to 0.0625
- gate_b_old: bfloat16 [8192, 512], P('dp'), may hold values from -0.0625 to 0.0625
- gate_a_old: bfloat16 [512, 14336], P(None, 'col'), may hold values from -0.25 to 0.25
- up_b_old: bfloat16 [8192, 512], P('dp'), may hold values from -0.0625 to 0.0625
- up_a_old: bfloat16 [512, 14336], P(None, 'col'), may hold values from -0.25 to 0.25
- gate_b_new: bfloat16 [8192, 512], P('dp'), may hold values from -0.0625 to 0.0625
- gate_right_factor: bfloat16 [512, 14336], P(None, 'col'), may hold values from -0.25 to 0.25
- up_b_new: bfloat16 [8192, 512], P('dp'), may hold values from -0.0625 to 0.0625
- up_right_factor: bfloat16 [512, 14336], P(None, 'col'), may hold values from -0.25 to 0.25
- hidden_grad: bfloat16 [2048, 14336], P('dp', 'col'), may hold values from -0.0625 to 0.0625
Outputs:
- merged_gate: bfloat16 [8192, 14336], P('dp', 'col')
- merged_up: bfloat16 [8192, 14336], P('dp', 'col')
- hidden: bfloat16 [2048, 14336], P('dp', 'col')
- gate_right_gradient: float32 [512, 14336], P('dp', 'col')
- up_right_gradient: float32 [512, 14336], P('dp', 'col')
- gate_left_gradient: float32 [8192, 512], P('dp', 'col')
- up_left_gradient: float32 [8192, 512], P('dp', 'col')
The draws below stay inside these ranges and needn't reach their ends.
All inputs are finite; a program needn't handle non-finite values.
Results may differ from the reference program's by a relative error of at most 0.028.
Values may be sent and summed in bfloat16 or wider, within the bound.
A program may use at most 128 MiB of HBM per device.

```python
import jax
import jax.numpy as jnp
from jax import lax

D = 8192
FF = 14336
R = 512
TOKENS = 2048
N_DP = 16


def with_spikes(drawn, stream_key, source, target, shards_of, factor):
    def block_of(axis_at):
        return (jnp.arange(drawn.shape[axis_at]) // (drawn.shape[axis_at] // shards_of)).reshape((-1,) + (1,) * (drawn.ndim - 1 - axis_at))

    one_side = jax.random.permutation(stream_key, shards_of)[block_of(target)]
    other_side = (block_of(target) + shards_of // 2) % shards_of
    return jnp.where((block_of(source) == one_side) | (block_of(source) == other_side), factor * drawn, drawn)


def block_scale(rng, dims, split, low, top_value):
    def one(axis_at, blocks):
        steps = jax.random.uniform(jax.random.fold_in(jax.random.fold_in(rng, 6), axis_at), (blocks,), jnp.float32, low / len(split), top_value / len(split))
        return jnp.repeat(jnp.exp(steps), dims[axis_at] // blocks).reshape((-1,) + (1,) * (len(dims) - axis_at - 1))

    gain = one(*split[0])
    for cut in split[1:]:
        gain = gain * one(*cut)
    return gain


def centred(rng, dims, scale, bound, cuts=(), held_as=jnp.bfloat16):
    array = scale * jax.random.normal(rng, dims, jnp.float32)
    if cuts:
        array = array * block_scale(rng, dims, cuts, -0.22, 0.18)
    return jnp.clip(array, -bound, bound).astype(held_as)


def noise_with(rng, extent, spread, most, pieces, heavy, held_as=jnp.bfloat16):
    drawn = spread * jax.random.normal(rng, extent, jnp.float32)
    if pieces:
        drawn = drawn * block_scale(rng, extent, pieces, -0.22, 0.18)
    return jnp.clip(with_spikes(drawn, jax.random.fold_in(rng, 3), *heavy), -most, most).astype(held_as)


def setup_inputs(seed: int = 0) -> dict:
    splits = jax.random.split(jax.random.key(seed), 13)
    tokens = noise_with(splits[0], (TOKENS, D), 1.0, 6.0, ((0, 8), (1, 16)), (1, 0, 16, 2.0))
    gate_weight = centred(splits[1], (D, FF), D ** -0.5, 0.0625, ((0, 16), (1, 8)))
    up_weight = centred(splits[2], (D, FF), D ** -0.5, 0.0625, ((0, 16), (1, 8)))
    gate_b_old = centred(splits[3], (D, R), D ** -0.5, 0.0625, ((0, 16),))
    gate_a_old = centred(splits[4], (R, FF), R ** -0.5, 0.25, ((1, 8),))
    up_b_old = centred(splits[5], (D, R), D ** -0.5, 0.0625, ((0, 16),))
    up_a_old = centred(splits[6], (R, FF), R ** -0.5, 0.25, ((1, 8),))
    gate_b_new = centred(splits[7], (D, R), D ** -0.5, 0.0625, ((0, 16),))
    gate_right_factor = centred(splits[8], (R, FF), R ** -0.5, 0.25, ((1, 8),))
    up_b_new = centred(splits[9], (D, R), D ** -0.5, 0.0625, ((0, 16),))
    up_right_factor = centred(splits[10], (R, FF), R ** -0.5, 0.25, ((1, 8),))
    hidden_grad = centred(splits[11], (TOKENS, FF), (TOKENS * 4) ** -0.5, 0.0625, ((0, 16), (1, 8)))
    return {"tokens": tokens, "gate_weight": gate_weight, "up_weight": up_weight, "gate_b_old": gate_b_old, "gate_a_old": gate_a_old, "up_b_old": up_b_old, "up_a_old": up_a_old, "gate_b_new": gate_b_new, "gate_right_factor": gate_right_factor, "up_b_new": up_b_new, "up_right_factor": up_right_factor, "hidden_grad": hidden_grad}


adapter_scale = 0.5


def merge_weight(weight_matrix, left, right):
    low_rank_input = jnp.dot(left, right, preferred_element_type=jnp.float32)
    return (weight_matrix.astype(jnp.float32) + adapter_scale * low_rank_input).astype(jnp.bfloat16)


def blocked_product(left, right):
    width = left.shape[1] // N_DP
    left_blocks = left.reshape(left.shape[0], N_DP, width).transpose(1, 0, 2)
    right_blocks = right.reshape(N_DP, width, right.shape[1])

    def add_block(carry, blocks):
        partial_value = jnp.dot(blocks[0], blocks[1], preferred_element_type=jnp.float32)
        rounded = lax.optimization_barrier(partial_value.astype(jnp.bfloat16))
        return carry + rounded.astype(jnp.float32), None

    start = jnp.zeros((left.shape[0], right.shape[1]), jnp.float32)
    total, unused = lax.scan(add_block, start, (left_blocks, right_blocks))
    return total


def reference(tokens, gate_weight, up_weight, gate_b_old, gate_a_old, up_b_old, up_a_old, gate_b_new, gate_right_factor, up_b_new, up_right_factor, hidden_grad):
    merged_gate = merge_weight(gate_weight, gate_b_old, gate_a_old)
    merged_up = merge_weight(up_weight, up_b_old, up_a_old)
    gate_linear = blocked_product(tokens, merged_gate)
    up_linear = blocked_product(tokens, merged_up)
    gate_low_rank = blocked_product(tokens, gate_b_new).astype(jnp.bfloat16)
    up_low_rank = blocked_product(tokens, up_b_new).astype(jnp.bfloat16)
    gate_activation = gate_linear + adapter_scale * jnp.dot(gate_low_rank, gate_right_factor, preferred_element_type=jnp.float32)
    up_activation = up_linear + adapter_scale * jnp.dot(up_low_rank, up_right_factor, preferred_element_type=jnp.float32)
    gate_sigma = jax.nn.sigmoid(gate_activation)
    active = gate_activation * gate_sigma
    hidden = (active * up_activation).astype(jnp.bfloat16)
    upstream = hidden_grad.astype(jnp.float32)
    gate_delta = (upstream * up_activation * gate_sigma * (1.0 + gate_activation * (1.0 - gate_sigma))).astype(jnp.bfloat16)
    up_delta = (upstream * active).astype(jnp.bfloat16)
    gate_right_gradient = adapter_scale * jnp.dot(gate_low_rank.T, gate_delta, preferred_element_type=jnp.float32)
    up_right_gradient = adapter_scale * jnp.dot(up_low_rank.T, up_delta, preferred_element_type=jnp.float32)
    gate_output_gradient = jnp.dot(gate_delta, gate_right_factor.T, preferred_element_type=jnp.float32).astype(jnp.bfloat16)
    up_output_gradient = jnp.dot(up_delta, up_right_factor.T, preferred_element_type=jnp.float32).astype(jnp.bfloat16)
    gate_left_gradient = adapter_scale * jnp.dot(tokens.T, gate_output_gradient, preferred_element_type=jnp.float32)
    up_left_gradient = adapter_scale * jnp.dot(tokens.T, up_output_gradient, preferred_element_type=jnp.float32)
    return (merged_gate, merged_up, hidden, gate_right_gradient, up_right_gradient, gate_left_gradient, up_left_gradient)
```

```python
import jax
import jax.numpy as jnp
from jax import lax
from jax.experimental import pallas as pl
from jax.experimental.pallas import tpu as pltpu
from jax.sharding import PartitionSpec as P

adapter_scale = 0.5
MESH = pl.DeviceIdType.MESH
NJ = 7
CW = 256
BF = jnp.bfloat16
F32 = jnp.float32


def f32(value):
    return value.astype(F32)


def dot(left, right, dims=((1,), (0,))):
    return lax.dot_general(left, right, (dims, ((), ())), preferred_element_type=F32)


def kernel(
    tokens, gate_w, up_w, gate_b_old, gate_a_old, up_b_old, up_a_old,
    gate_b_new, gate_right, up_b_new, up_right, hidden_grad,
    merged_gate, merged_up, hidden, gate_rg, up_rg, gate_lg, up_lg,
    tok, wts, raw, a_old, right, fac, low_w, hgrad,
    gp, gxo, gxn, gz, up, uz, uxo, uxn,
    lp, lxo, lxn, lz,
    rgp, rgxo, rgxn, rgz, rup, ruz, ruxo, ruxn,
    delta, low_t, low_sib, low_sel,
    g_acc, g_send, g_recv, g_all, l_recv, l_send,
    in_sem, tok_in_sem, mo_sem, sib_s, sib_r, ag_s, ag_r,
    gp_s, gp_r, up_s, up_r, lp_s, lp_r, rgp_s, rgp_r, rup_s, rup_r,
    dl_s, dl_r, col_s, col_r, gcol_s, gcol_r, gdp_s, gdp_r,
):
    d = lax.axis_index("dp")
    c = lax.axis_index("col")
    q, k = d // 2, d % 2
    x, z = q // 2, q % 2
    zh, y = c // 4, c % 4
    xr, xl, xo = (x + 1) % 4, (x + 3) % 4, (x + 2) % 4
    yr, yl, yo = (y + 1) % 4, (y + 3) % 4, (y + 2) % 4

    def at_chip(xx, zz):
        return ((xx * 2 + zz) * 2 + k, c)

    def at_col(hh, yy):
        return (d, hh * 4 + yy)

    sibling = (q * 2 + 1 - k, c)
    to_right, to_left, to_z = at_chip(xr, z), at_chip(xl, z), at_chip(x, 1 - z)

    def remote(src, dst, send, recv, device):
        return pltpu.make_async_remote_copy(
            src_ref=src, dst_ref=dst, send_sem=send, recv_sem=recv,
            device_id=device, device_id_type=MESH,
        )

    weights = (gate_w, up_w, gate_a_old, up_a_old, gate_right, up_right)

    def load(n, j):
        held = (raw, raw, a_old, a_old, right, right)[n]
        cols = pl.ds(pl.multiple_of(j * CW, CW), CW)
        return pltpu.make_async_copy(weights[n].at[:, cols], held.at[j, n % 2], in_sem.at[j, n])

    factors = (gate_b_old, up_b_old, gate_b_new, up_b_new)

    def load_factor(n):
        return pltpu.make_async_copy(factors[n], fac.at[n], tok_in_sem.at[n])

    own_tokens = pltpu.make_async_copy(
        tokens.at[pl.ds(pl.multiple_of(k * 128, 128), 128)],
        tok.at[c, :, pl.ds(0, 512)], tok_in_sem.at[4],
    )
    load_hgrad = pltpu.make_async_copy(hidden_grad, hgrad, tok_in_sem.at[5])
    own_tokens.start()
    for n in range(4):
        load_factor(n).start()

    @pl.loop(0, NJ)
    def _(j):
        for n in range(6):
            load(n, j).start()

    load_hgrad.start()

    barrier = pltpu.get_barrier_semaphore()

    def greet(device):
        pl.semaphore_signal(barrier, inc=1, device_id=device, device_id_type=MESH)

    greet(sibling)
    for step in range(1, 8):
        greet((((q + step) % 8) * 2 + k, c))
        greet((d, (c + step) % 8))
    pl.semaphore_wait(barrier, 15)

    sib_tokens = remote(
        tokens.at[pl.ds(pl.multiple_of((1 - k) * 128, 128), 128)],
        tok.at[c, :, pl.ds(512, 512)], sib_s.at[0], sib_r.at[0], sibling,
    )
    sib_tokens.start()

    def block(n, slot, half, device):
        ref = tok.at[slot] if half is None else tok.at[slot, pl.ds(64 * half, 64)]
        return remote(ref, ref, ag_s.at[n], ag_r.at[slot, half or 0], device)

    own, other = zh * 4, (1 - zh) * 4
    to_yr, to_yl, to_zo = at_col(zh, yr), at_col(zh, yl), at_col(1 - zh, y)
    ag = (
        block(0, own + y, None, to_yr), block(1, own + y, None, to_yl), block(2, own + y, None, to_zo),
        block(3, own + yl, 0, to_yr), block(4, own + yr, 1, to_yl),
        block(5, other + y, None, to_yr), block(6, other + y, None, to_yl),
        block(7, other + yl, 0, to_yr), block(8, other + yr, 1, to_yl),
    )

    def ag_wait(slot, half=None):
        block(0, slot, half, to_yr).wait_recv()

    def send_weights(j):
        return remote(wts.at[j, pl.ds(0, 512)], wts.at[j, pl.ds(512, 512)], sib_s.at[2 + j], sib_r.at[2 + j], sibling)

    def store_merged(j, mat):
        cols = pl.ds(pl.multiple_of(j * CW, CW), CW)
        return pltpu.make_async_copy(raw.at[j, mat], (merged_gate, merged_up)[mat].at[:, cols], mo_sem.at[j, mat])

    def merge(j):
        for n in range(6):
            load(n, j).wait()
        for mat in range(2):
            merged = f32(raw[j, mat]) + adapter_scale * dot(fac[mat], a_old[j, mat])
            merged = merged.astype(BF)
            raw[j, mat] = merged
            folded = f32(merged) + adapter_scale * dot(fac[2 + mat], right[j, mat])
            wts[j, 0:512, mat * CW:(mat + 1) * CW] = folded.astype(BF)
        send_weights(j).start()
        for mat in range(2):
            store_merged(j, mat).start()

    own_tokens.wait()
    sib_tokens.wait_recv()
    for n in range(3):
        ag[n].start()

    for n in range(4):
        load_factor(n).wait()
    low_cols = pl.ds(pl.multiple_of((c % 4) * 128, 128), 128)
    low_w[0:512, :] = jnp.where(c < 4, fac[2, :, low_cols], fac[3, :, low_cols])
    send_low_w = remote(low_w.at[pl.ds(0, 512)], low_w.at[pl.ds(512, 512)], sib_s.at[1], sib_r.at[1], sibling)
    send_low_w.start()

    pl.loop(0, 4)(merge)
    ag_wait(own + yl)
    ag[3].start()
    ag_wait(own + yr)
    ag[4].start()
    ag_wait(other + y)
    ag[5].start()
    ag[6].start()
    pl.loop(4, NJ)(merge)
    ag_wait(other + yl)
    ag[7].start()
    ag_wait(other + yr)
    ag[8].start()
    send_low_w.wait_recv()
    for slot in (own + yo, other + yo):
        for half in range(2):
            ag_wait(slot, half)

    class XFirst:
        def __init__(self, part, opp, near, last, send, recv):
            self.part, self.opp, self.near, self.last = part, opp, near, last
            self.send, self.recv = send, recv

        def copy(self, j, n):
            part, opp, near = self.part, self.opp, self.near
            pairs = (
                (part.at[j, xo, 0], opp.at[j, 0], to_right),
                (part.at[j, xo, 1], opp.at[j, 1], to_left),
                (part.at[j, xr, 1], near.at[j, 0, 1], to_right),
                (part.at[j, xl, 0], near.at[j, 1, 0], to_left),
                (part.at[j, xr, 0], near.at[j, 0, 0], to_right),
                (part.at[j, xl, 1], near.at[j, 1, 1], to_left),
                (part.at[j, x, 1 - z], self.last.at[j], to_z),
            )
            return remote(pairs[n][0], pairs[n][1], self.send.at[j, n], self.recv.at[j, n], pairs[n][2])

        def step1(self, j):
            for n in range(4):
                self.copy(j, n).start()

        def step2(self, j):
            part = self.part
            self.copy(j, 0).wait_recv()
            part[j, xr, 0] = (f32(part[j, xr, 0]) + f32(self.opp[j, 0])).astype(BF)
            self.copy(j, 4).start()
            self.copy(j, 1).wait_recv()
            part[j, xl, 1] = (f32(part[j, xl, 1]) + f32(self.opp[j, 1])).astype(BF)
            self.copy(j, 5).start()

        def step3(self, j):
            for n in range(2, 6):
                self.copy(j, n).wait_recv()
            near = self.near
            self.part[j, x, 1 - z] = (
                f32(self.part[j, x, 1 - z]) + f32(near[j, 0, 1 - z]) + f32(near[j, 1, 1 - z])
            ).astype(BF)
            self.copy(j, 6).start()

        def final(self, j):
            self.copy(j, 6).wait_recv()
            near = self.near
            return f32(self.part[j, x, z]) + f32(near[j, 0, z]) + f32(near[j, 1, z]) + f32(self.last[j])

        def drain(self, j):
            for n in range(7):
                self.copy(j, n).wait_send()

    class ZFirst:
        def __init__(self, part, first, opp, near, send, recv):
            self.part, self.first, self.opp, self.near = part, first, opp, near
            self.send, self.recv = send, recv
            self.rows = part.shape[3] // 2

        def copy(self, j, n):
            low, high = pl.ds(0, self.rows), pl.ds(self.rows, self.rows)
            part, opp, near = self.part, self.opp, self.near
            pairs = (
                (part.at[j, :, 1 - z], self.first.at[j], to_z),
                (part.at[j, xo, z, low], opp.at[j, 0], to_right),
                (part.at[j, xo, z, high], opp.at[j, 1], to_left),
                (part.at[j, xr, z, high], near.at[j, 0, high], to_right),
                (part.at[j, xl, z, low], near.at[j, 1, low], to_left),
                (part.at[j, xr, z, low], near.at[j, 0, low], to_right),
                (part.at[j, xl, z, high], near.at[j, 1, high], to_left),
            )
            return remote(pairs[n][0], pairs[n][1], self.send.at[j, n], self.recv.at[j, n], pairs[n][2])

        def step1(self, j):
            self.copy(j, 0).start()

        def step2(self, j):
            self.copy(j, 0).wait_recv()
            part = self.part
            for xx in (xo, xr, xl, x):
                part[j, xx, z] = (f32(part[j, xx, z]) + f32(self.first[j, xx])).astype(BF)
            for n in range(1, 5):
                self.copy(j, n).start()

        def step3(self, j):
            part, n = self.part, self.rows
            self.copy(j, 1).wait_recv()
            part[j, xr, z, 0:n] = (f32(part[j, xr, z, 0:n]) + f32(self.opp[j, 0])).astype(BF)
            self.copy(j, 5).start()
            self.copy(j, 2).wait_recv()
            part[j, xl, z, n:2 * n] = (f32(part[j, xl, z, n:2 * n]) + f32(self.opp[j, 1])).astype(BF)
            self.copy(j, 6).start()

        def final(self, j):
            for n in range(3, 7):
                self.copy(j, n).wait_recv()
            return f32(self.part[j, x, z]) + f32(self.near[j, 0]) + f32(self.near[j, 1])

        def drain(self, j):
            for n in range(7):
                self.copy(j, n).wait_send()

    gate_sum = XFirst(gp, gxo, gxn, gz, gp_s, gp_r)
    up_sum = ZFirst(up, uz, uxo, uxn, up_s, up_r)
    low_sum = XFirst(lp, lxo, lxn, lz, lp_s, lp_r)
    rg_sum = XFirst(rgp, rgxo, rgxn, rgz, rgp_s, rgp_r)
    ru_sum = ZFirst(rup, ruz, ruxo, ruxn, rup_s, rup_r)

    def low_copy(step):
        return remote(low_t.at[c], low_t.at[c], col_s.at[step], col_r.at[c], (d, (c + step) % 8))

    def low_wait(step):
        slot = (c + step) % 8
        remote(low_t.at[slot], low_t.at[slot], col_s.at[0], col_r.at[slot], sibling).wait_recv()

    send_low_sel = remote(low_t.at[:, :, 1 - k], low_sib, sib_s.at[9], sib_r.at[9], sibling)

    def low_start():
        for h in range(2):
            rows = tok[4 * h:4 * h + 4].reshape(512, 1024)
            lp[0, 2 * h:2 * h + 2] = dot(rows, low_w[...]).astype(BF).reshape(2, 2, 128, 128)
        low_sum.step1(0)

    def low_share():
        low_t[c] = low_sum.final(0).T.astype(BF).reshape(2, 2, 32, 128)
        for step in range(1, 8):
            low_copy(step).start()

    def low_swap():
        for step in range(1, 8):
            low_wait(step)
        send_low_sel.start()

    def low_pick():
        send_low_sel.wait_recv()
        for mat in range(2):
            low_sel[mat, :, 0:128] = low_t[4 * mat:4 * mat + 4, :, k].reshape(256, 128)
            low_sel[mat, :, 128:256] = low_sib[4 * mat:4 * mat + 4].reshape(256, 128)

    def products(j):
        send_weights(j).wait_recv()
        for h in range(2):
            rows = tok[4 * h:4 * h + 4].reshape(512, 1024)
            terms = dot(rows, wts[j]).astype(BF)
            gp[j, 2 * h:2 * h + 2] = terms[:, 0:CW].reshape(2, 2, 128, CW)
            up[j, 2 * h:2 * h + 2] = terms[:, CW:2 * CW].reshape(2, 2, 128, CW)
        gate_sum.step1(j)
        up_sum.step1(j)

    def send_delta(j):
        return remote(delta.at[j, :, 0], delta.at[j, :, 1], dl_s.at[j], dl_r.at[j], sibling)

    def activate(j):
        cols = pl.ds(pl.multiple_of(j * CW, CW), CW)
        gate = gate_sum.final(j)
        upv = up_sum.final(j)
        sg = 1.0 / (1.0 + jnp.exp(-gate))
        active = gate * sg
        hidden[:, cols] = (active * upv).astype(BF)
        upstream = f32(hgrad[:, cols])
        delta[j, 0, 0] = (upstream * upv * sg * (1.0 + gate * (1.0 - sg))).astype(BF)
        delta[j, 1, 0] = (upstream * active).astype(BF)
        send_delta(j).start()
        for mat in range(2):
            g_acc[mat] += dot(right[j, mat], delta[j, mat, 0], ((1,), (1,)))

    def right_products(j):
        send_delta(j).wait_recv()
        for mat in range(2):
            terms = dot(low_sel[mat], delta[j, mat].reshape(256, CW)).astype(BF)
            (rgp, rup)[mat][j] = terms.reshape(4, 2, 32, CW)
        rg_sum.step1(j)
        ru_sum.step1(j)

    def right_final(j):
        cols = pl.ds(pl.multiple_of(j * CW, CW), CW)
        gate_rg[:, cols] = adapter_scale * rg_sum.final(j)
        up_rg[:, cols] = adapter_scale * ru_sum.final(j)

    def g_col(step):
        peer = (c + step) % 8
        return remote(g_send.at[peer], g_recv.at[c], gcol_s.at[step], gcol_r.at[c], (d, peer))

    def g_col_wait(step):
        slot = (c + step) % 8
        remote(g_send.at[slot], g_recv.at[slot], gcol_s.at[0], gcol_r.at[slot], sibling).wait_recv()

    def g_dp(step):
        return remote(g_all.at[q], g_all.at[q], gdp_s.at[step], gdp_r.at[q], (((q + step) % 8) * 2 + k, c))

    def g_dp_wait(step):
        slot = (q + step) % 8
        remote(g_all.at[slot], g_all.at[slot], gdp_s.at[0], gdp_r.at[slot], sibling).wait_recv()

    send_left = remote(l_send.at[:, pl.ds(512, 512)], l_recv, sib_s.at[10], sib_r.at[10], sibling)

    def g_start():
        for mat in range(2):
            g_send[:, 64 * mat:64 * mat + 64] = g_acc[mat].astype(BF).reshape(8, 64, 128)
        for step in range(1, 8):
            g_col(step).start()

    def g_share():
        total = f32(g_send[c])
        for step in range(1, 8):
            g_col_wait(step)
            total = total + f32(g_recv[(c + step) % 8])
        g_all[q] = total.astype(BF)
        for step in range(1, 8):
            g_dp(step).start()

    def left_products():
        for step in range(1, 8):
            g_dp_wait(step)
        g = jnp.concatenate([g_all[n] for n in range(8)], axis=1)
        for h in range(2):
            cols = slice(512 * h, 512 * h + 512)
            l_send[:, cols] = dot(g, tok[:, :, cols].reshape(1024, 512))
        send_left.start()

    def left_final():
        send_left.wait_recv()
        total = (adapter_scale * (l_send[:, 0:512] + l_recv[...])).T
        gate_lg[...] = total[:, 0:64]
        up_lg[...] = total[:, 64:128]

    low_start()
    load_hgrad.wait()
    g_acc[...] = jnp.zeros_like(g_acc)

    @pl.loop(0, NJ + 7)
    def _(i):
        def lag(n, *stages):
            @pl.when((i >= n) & (i < n + NJ))
            def _():
                for stage in stages:
                    stage(i - n)

        def once(n, stage):
            @pl.when(i == n)
            def _():
                stage()

        lag(0, products)
        once(0, lambda: low_sum.step2(0))
        lag(1, gate_sum.step2, up_sum.step2)
        once(1, lambda: low_sum.step3(0))
        lag(2, gate_sum.step3, up_sum.step3)
        once(2, low_share)
        lag(3, activate)
        once(3, low_swap)
        once(4, low_pick)
        once(9, g_start)
        lag(4, right_products)
        lag(5, rg_sum.step2, ru_sum.step2)
        once(10, g_share)
        lag(6, rg_sum.step3, ru_sum.step3)
        once(11, left_products)
        lag(7, right_final)
        once(12, left_final)

    @pl.loop(0, NJ)
    def _(j):
        for total in (gate_sum, up_sum, rg_sum, ru_sum):
            total.drain(j)
        send_weights(j).wait_send()
        send_delta(j).wait_send()
        for mat in range(2):
            store_merged(j, mat).wait()

    low_sum.drain(0)
    sib_tokens.wait_send()
    send_low_w.wait_send()
    send_low_sel.wait_send()
    send_left.wait_send()
    for copy in ag:
        copy.wait_send()
    for step in range(1, 8):
        low_copy(step).wait_send()
        g_col(step).wait_send()
        g_dp(step).wait_send()


def local(*args):
    hbm = pl.BlockSpec(memory_space=pl.ANY)
    vmem = pl.BlockSpec(memory_space=pltpu.VMEM)

    def bf(*shape):
        return pltpu.VMEM(shape, BF)

    def fl(*shape):
        return pltpu.VMEM(shape, F32)

    def dma(*shape):
        return pltpu.SemaphoreType.DMA(shape)

    def x_first(n, rows, width):
        return [bf(n, 4, 2, rows, width), bf(n, 2, rows, width), bf(n, 2, 2, rows, width), bf(n, rows, width)]

    def z_first(n, rows, width):
        return [bf(n, 4, 2, rows, width), bf(n, 4, rows, width), bf(n, 2, rows // 2, width), bf(n, 2, rows, width)]

    scratch = [
        bf(8, 128, 1024), bf(NJ, 1024, 2 * CW), bf(NJ, 2, 512, CW), bf(NJ, 2, 512, CW), bf(NJ, 2, 512, CW),
        bf(4, 512, 512), bf(1024, 128), bf(128, NJ * CW),
        *x_first(NJ, 128, CW), *z_first(NJ, 128, CW),
        *x_first(1, 128, 128),
        *x_first(NJ, 32, CW), *z_first(NJ, 32, CW),
        bf(NJ, 2, 2, 128, CW), bf(8, 2, 2, 32, 128), bf(8, 2, 32, 128), bf(2, 256, 256),
        fl(2, 512, 128), bf(8, 128, 128), bf(8, 128, 128), bf(8, 128, 128), fl(128, 512), fl(128, 1024),
        dma(NJ, 6), dma(6), dma(NJ, 2), dma(11), dma(11), dma(9), dma(8, 2),
        dma(NJ, 7), dma(NJ, 7), dma(NJ, 7), dma(NJ, 7), dma(1, 7), dma(1, 7),
        dma(NJ, 7), dma(NJ, 7), dma(NJ, 7), dma(NJ, 7),
        dma(NJ), dma(NJ), dma(8), dma(8), dma(8), dma(8), dma(8), dma(8),
    ]
    return pl.pallas_call(
        kernel,
        out_shape=(
            jax.ShapeDtypeStruct((512, 1792), BF),
            jax.ShapeDtypeStruct((512, 1792), BF),
            jax.ShapeDtypeStruct((128, 1792), BF),
            jax.ShapeDtypeStruct((32, 1792), F32),
            jax.ShapeDtypeStruct((32, 1792), F32),
            jax.ShapeDtypeStruct((512, 64), F32),
            jax.ShapeDtypeStruct((512, 64), F32),
        ),
        in_specs=[hbm] * 12,
        out_specs=(hbm, hbm, vmem, vmem, vmem, vmem, vmem),
        scratch_shapes=scratch,
        compiler_params=pltpu.CompilerParams(
            collective_id=0, has_side_effects=True, vmem_limit_bytes=60 * 1024 * 1024
        ),
        cost_estimate=pl.CostEstimate(flops=14_000_000_000, bytes_accessed=24_000_000, transcendentals=230_000),
    )(*args)


def solution(mesh):
    rows, cols = P("dp", None), P(None, "col")
    both = P("dp", "col")
    return jax.shard_map(
        local,
        mesh=mesh,
        in_specs=(P("col", "dp"), both, both, rows, cols, rows, cols, rows, cols, rows, cols, both),
        out_specs=(both,) * 7,
        check_vma=False,
    )
```

```python
import jax
import jax.numpy as jnp
from jax import lax
from jax.experimental import pallas as pl
from jax.experimental.pallas import tpu as pltpu
from jax.sharding import PartitionSpec as P

adapter_scale = 0.5
MESH = pl.DeviceIdType.MESH
NJ = 7
CW = 256
BF = jnp.bfloat16
F32 = jnp.float32
VMEM_LIMIT = 54 * 1024 * 1024


def f32(value):
    return value.astype(F32)


def dot(left, right, dims=((1,), (0,))):
    return lax.dot_general(left, right, (dims, ((), ())), preferred_element_type=F32)


def kernel(
    tokens, gate_w, up_w, gate_b_old, gate_a_old, up_b_old, up_a_old,
    gate_b_new, gate_right, up_b_new, up_right, hidden_grad,
    merged_gate, merged_up, hidden, gate_rg, up_rg, gate_lg, up_lg,
    tok, wts, raw, a_old, right, fac, low_w, hgrad,
    gp, gxo, gxn, gz, up, uz, uxo, uxn,
    lp, lxo, lxn, lz,
    rp, rxo, rxn, rz,
    delta, low_t, low_sib, low_sel,
    g_acc, g_send, g_recv, g_all, l_recv, l_send,
    in_sem, tok_in_sem, sib_s, sib_r, ag_s, ag_r,
    gp_s, gp_r, up_s, up_r, lp_s, lp_r, rp_s, rp_r,
    dl_s, dl_r, col_s, col_r, gcol_s, gcol_r, gdp_s, gdp_r,
):
    d = lax.axis_index("dp")
    c = lax.axis_index("col")
    q, k = d // 2, d % 2
    x, z = q // 2, q % 2
    zh, y = c // 4, c % 4
    xr, xl, xo = (x + 1) % 4, (x + 3) % 4, (x + 2) % 4
    yr, yl, yo = (y + 1) % 4, (y + 3) % 4, (y + 2) % 4

    def at_chip(xx, zz):
        return ((xx * 2 + zz) * 2 + k, c)

    def at_col(hh, yy):
        return (d, hh * 4 + yy)

    sibling = (q * 2 + 1 - k, c)
    to_right, to_left, to_z = at_chip(xr, z), at_chip(xl, z), at_chip(x, 1 - z)

    def remote(src, dst, send, recv, device):
        return pltpu.make_async_remote_copy(
            src_ref=src, dst_ref=dst, send_sem=send, recv_sem=recv,
            device_id=device, device_id_type=MESH,
        )

    weights = (gate_w, up_w, gate_a_old, up_a_old, gate_right, up_right)

    def load(n, j):
        held = (raw, raw, a_old, a_old, right, right)[n]
        cols = pl.ds(pl.multiple_of(j * CW, CW), CW)
        return pltpu.make_async_copy(weights[n].at[:, cols], held.at[j, n % 2], in_sem.at[j, n])

    factors = (gate_b_old, up_b_old, gate_b_new, up_b_new)

    def load_factor(n):
        return pltpu.make_async_copy(factors[n], fac.at[n], tok_in_sem.at[n])

    own_tokens = pltpu.make_async_copy(
        tokens.at[pl.ds(pl.multiple_of(k * 128, 128), 128)],
        tok.at[c, :, pl.ds(0, 512)], tok_in_sem.at[4],
    )
    load_hgrad = pltpu.make_async_copy(hidden_grad, hgrad, tok_in_sem.at[5])
    barrier = pltpu.get_barrier_semaphore()

    def greet(device):
        pl.semaphore_signal(barrier, inc=1, device_id=device, device_id_type=MESH)

    to_yr, to_yl, to_zo = at_col(zh, yr), at_col(zh, yl), at_col(1 - zh, y)
    greet(sibling)
    for there in (to_yr, to_yl, to_zo):
        greet((q * 2 + 1 - k, there[1]))
    for step in range(1, 8):
        greet((((q + step) % 8) * 2 + k, c))
        greet((d, (c + step) % 8))
    own_tokens.start()
    pl.semaphore_wait(barrier, 18)

    own, other = zh * 4, (1 - zh) * 4

    def rows_of(core, h):
        return tokens.at[pl.ds(pl.multiple_of(core * 128 + 64 * h, 64), 64)]

    def own_width(n, device, h, slot=c):
        dst = tok.at[slot, pl.ds(64 * h, 64), pl.ds(0, 512)]
        return remote(rows_of(k, h), dst, ag_s.at[12 * h + n], ag_r.at[slot, h, 0], device)

    def sib_width(n, device, h, slot=c):
        dst = tok.at[slot, pl.ds(64 * h, 64), pl.ds(512, 512)]
        there = (q * 2 + 1 - k, device[1])
        return remote(rows_of(1 - k, h), dst, ag_s.at[12 * h + n], ag_r.at[slot, h, 1], there)

    def block(n, slot, h, part, device):
        ref = tok.at[slot, pl.ds(64 * h, 64) if part is None else pl.ds(64 * h + 32 * part, 32)]
        return remote(ref, ref, ag_s.at[12 * h + n], ag_r.at[slot, h, part or 0], device)

    def direct(h):
        return (
            own_width(0, to_yr, h), own_width(1, to_yl, h), sib_width(2, to_yr, h), sib_width(3, to_yl, h),
            own_width(4, to_zo, h), sib_width(5, to_zo, h), sib_width(6, (d, c), h),
        )

    def passed(h):
        return (
            block(7, own + yl, h, 0, to_yr), block(8, own + yr, h, 1, to_yl),
            block(9, other + y, h, None, to_yr), block(10, other + y, h, None, to_yl),
            block(11, own + yo, h, None, to_zo),
        )

    def wait_direct(slot, h):
        own_width(0, to_yr, h, slot).wait_recv()
        sib_width(0, to_yr, h, slot).wait_recv()

    def pass_on(h):
        copies = passed(h)
        wait_direct(own + yl, h)
        copies[0].start()
        wait_direct(own + yr, h)
        copies[1].start()
        wait_direct(other + y, h)
        copies[2].start()
        copies[3].start()

    def pass_far(h):
        for part in range(2):
            block(0, own + yo, h, part, to_yr).wait_recv()
        passed(h)[4].start()

    def wait_rest(h):
        sib_width(0, to_yr, h).wait_recv()
        for slot in (other + yl, other + yr, other + yo):
            block(0, slot, h, None, to_yr).wait_recv()

    for copy in direct(0):
        copy.start()
    for n in range(4):
        load_factor(n).start()

    @pl.loop(0, NJ)
    def _(j):
        for n in range(6):
            load(n, j).start()

    load_hgrad.start()

    def send_weights(j):
        return remote(wts.at[j, pl.ds(0, 512)], wts.at[j, pl.ds(512, 512)], sib_s.at[2 + j], sib_r.at[2 + j], sibling)

    def merge(j):
        cols = pl.ds(pl.multiple_of(j * CW, CW), CW)
        for n in range(6):
            load(n, j).wait()
        for mat in range(2):
            merged = f32(raw[j, mat]) + adapter_scale * dot(fac[mat], a_old[j, mat])
            merged = merged.astype(BF)
            (merged_gate, merged_up)[mat][:, cols] = merged
            folded = f32(merged) + adapter_scale * dot(fac[2 + mat], right[j, mat])
            wts[j, 0:512, mat * CW:(mat + 1) * CW] = folded.astype(BF)
        send_weights(j).start()

    for n in range(4):
        load_factor(n).wait()
    low_cols = pl.ds(pl.multiple_of((c % 4) * 128, 128), 128)
    low_w[0:512, :] = jnp.where(c < 4, fac[2, :, low_cols], fac[3, :, low_cols])
    send_low_w = remote(low_w.at[pl.ds(0, 512)], low_w.at[pl.ds(512, 512)], sib_s.at[1], sib_r.at[1], sibling)
    send_low_w.start()

    class Sum:
        def parts(self, n):
            return (0, 1) if self.halves and n in self.first_copies else (None,)

        def copy(self, j, n, h=None):
            src, dst, device = self.pairs(j, slice(None) if h is None else pl.ds(64 * h, 64))[n]
            sem = n + 7 if h == 1 else n
            return remote(src, dst, self.send.at[j, sem], self.recv.at[j, sem], device)

        def step1(self, j, h=None):
            for n in self.first_copies:
                self.copy(j, n, h).start()

        def wait(self, j, n):
            for h in self.parts(n):
                self.copy(j, n, h).wait_recv()

        def drain(self, j):
            for n in range(7):
                for h in self.parts(n):
                    self.copy(j, n, h).wait_send()

    class XFirst(Sum):
        first_copies = (0, 1, 2, 3)

        def __init__(self, part, opp, near, last, send, recv, halves=False):
            self.part, self.opp, self.near, self.last = part, opp, near, last
            self.send, self.recv, self.halves = send, recv, halves

        def pairs(self, j, rows):
            part, opp, near = self.part, self.opp, self.near
            return (
                (part.at[j, xo, 0, rows], opp.at[j, 0, rows], to_right),
                (part.at[j, xo, 1, rows], opp.at[j, 1, rows], to_left),
                (part.at[j, xr, 1, rows], near.at[j, 0, 1, rows], to_right),
                (part.at[j, xl, 0, rows], near.at[j, 1, 0, rows], to_left),
                (part.at[j, xr, 0], near.at[j, 0, 0], to_right),
                (part.at[j, xl, 1], near.at[j, 1, 1], to_left),
                (part.at[j, x, 1 - z], self.last.at[j], to_z),
            )

        def step2(self, j):
            part = self.part
            self.wait(j, 0)
            part[j, xr, 0] = (f32(part[j, xr, 0]) + f32(self.opp[j, 0])).astype(BF)
            self.copy(j, 4).start()
            self.wait(j, 1)
            part[j, xl, 1] = (f32(part[j, xl, 1]) + f32(self.opp[j, 1])).astype(BF)
            self.copy(j, 5).start()

        def step3(self, j):
            for n in range(2, 6):
                self.wait(j, n)
            near = self.near
            self.part[j, x, 1 - z] = (
                f32(self.part[j, x, 1 - z]) + f32(near[j, 0, 1 - z]) + f32(near[j, 1, 1 - z])
            ).astype(BF)
            self.copy(j, 6).start()

        def final(self, j):
            self.wait(j, 6)
            near = self.near
            return f32(self.part[j, x, z]) + f32(near[j, 0, z]) + f32(near[j, 1, z]) + f32(self.last[j])

    class ZFirst(Sum):
        first_copies = (0,)

        def __init__(self, part, first, opp, near, send, recv, halves=False):
            self.part, self.first, self.opp, self.near = part, first, opp, near
            self.send, self.recv, self.halves = send, recv, halves
            self.rows = part.shape[3] // 2

        def pairs(self, j, rows):
            low, high = pl.ds(0, self.rows), pl.ds(self.rows, self.rows)
            part, opp, near = self.part, self.opp, self.near
            return (
                (part.at[j, :, 1 - z, rows], self.first.at[j, :, rows], to_z),
                (part.at[j, xo, z, low], opp.at[j, 0], to_right),
                (part.at[j, xo, z, high], opp.at[j, 1], to_left),
                (part.at[j, xr, z, high], near.at[j, 0, high], to_right),
                (part.at[j, xl, z, low], near.at[j, 1, low], to_left),
                (part.at[j, xr, z, low], near.at[j, 0, low], to_right),
                (part.at[j, xl, z, high], near.at[j, 1, high], to_left),
            )

        def step2(self, j):
            self.wait(j, 0)
            part = self.part
            for xx in (xo, xr, xl, x):
                part[j, xx, z] = (f32(part[j, xx, z]) + f32(self.first[j, xx])).astype(BF)
            for n in range(1, 5):
                self.copy(j, n).start()

        def step3(self, j):
            part, n = self.part, self.rows
            self.wait(j, 1)
            part[j, xr, z, 0:n] = (f32(part[j, xr, z, 0:n]) + f32(self.opp[j, 0])).astype(BF)
            self.copy(j, 5).start()
            self.wait(j, 2)
            part[j, xl, z, n:2 * n] = (f32(part[j, xl, z, n:2 * n]) + f32(self.opp[j, 1])).astype(BF)
            self.copy(j, 6).start()

        def final(self, j):
            for n in range(3, 7):
                self.wait(j, n)
            return f32(self.part[j, x, z]) + f32(self.near[j, 0]) + f32(self.near[j, 1])

    gate_sum = XFirst(gp, gxo, gxn, gz, gp_s, gp_r, halves=True)
    up_sum = ZFirst(up, uz, uxo, uxn, up_s, up_r, halves=True)
    low_sum = XFirst(lp, lxo, lxn, lz, lp_s, lp_r)
    right_sum = XFirst(rp, rxo, rxn, rz, rp_s, rp_r)

    def low_copy(step):
        return remote(low_t.at[c], low_t.at[c], col_s.at[step], col_r.at[c], (d, (c + step) % 8))

    def low_wait(step):
        slot = (c + step) % 8
        remote(low_t.at[slot], low_t.at[slot], col_s.at[0], col_r.at[slot], sibling).wait_recv()

    send_low_sel = remote(low_t.at[:, :, 1 - k], low_sib, sib_s.at[9], sib_r.at[9], sibling)

    def low_start():
        for h in range(2):
            rows = tok[4 * h:4 * h + 4].reshape(512, 1024)
            lp[0, 2 * h:2 * h + 2] = dot(rows, low_w[...]).astype(BF).reshape(2, 2, 128, 128)
        low_sum.step1(0)

    def low_share():
        low_t[c] = low_sum.final(0).T.astype(BF).reshape(2, 2, 32, 128)
        for step in range(1, 8):
            low_copy(step).start()

    def low_swap():
        for step in range(1, 8):
            low_wait(step)
        send_low_sel.start()

    def low_pick():
        send_low_sel.wait_recv()
        for mat in range(2):
            low_sel[mat, :, 0:128] = low_t[4 * mat:4 * mat + 4, :, k].reshape(256, 128)
            low_sel[mat, :, 128:256] = low_sib[4 * mat:4 * mat + 4].reshape(256, 128)

    def products(j, h):
        part = slice(64 * h, 64 * h + 64)
        terms = dot(tok[:, part].reshape(512, 1024), wts[j]).astype(BF)
        gp[j, :, :, part] = terms[:, 0:CW].reshape(4, 2, 64, CW)
        up[j, :, :, part] = terms[:, CW:2 * CW].reshape(4, 2, 64, CW)

    def rest_of_products(j):
        products(j, 1)
        gate_sum.step1(j, 1)
        up_sum.step1(j, 1)

        @pl.when(j > 2)
        def _():
            up_sum.step1(j, 0)

    def send_delta(j):
        return remote(delta.at[j, :, 0], delta.at[j, :, 1], dl_s.at[j], dl_r.at[j], sibling)

    def activate(j):
        cols = pl.ds(pl.multiple_of(j * CW, CW), CW)
        gate = gate_sum.final(j)
        upv = up_sum.final(j)
        sg = 1.0 / (1.0 + jnp.exp(-gate))
        active = gate * sg
        hidden[:, cols] = (active * upv).astype(BF)
        upstream = f32(hgrad[:, cols])
        delta[j, 0, 0] = (upstream * upv * sg * (1.0 + gate * (1.0 - sg))).astype(BF)
        delta[j, 1, 0] = (upstream * active).astype(BF)
        send_delta(j).start()
        for mat in range(2):
            g_acc[mat] += dot(right[j, mat], delta[j, mat, 0], ((1,), (1,)))

    def right_products(j):
        send_delta(j).wait_recv()
        for mat in range(2):
            terms = dot(low_sel[mat], delta[j, mat].reshape(256, CW)).astype(BF)
            rp[j, :, :, 32 * mat:32 * mat + 32] = terms.reshape(4, 2, 32, CW)
        right_sum.step1(j)

    def right_final(j):
        cols = pl.ds(pl.multiple_of(j * CW, CW), CW)
        total = adapter_scale * right_sum.final(j)
        gate_rg[:, cols] = total[0:32]
        up_rg[:, cols] = total[32:64]

    def g_col(step):
        peer = (c + step) % 8
        return remote(g_send.at[peer], g_recv.at[c], gcol_s.at[step], gcol_r.at[c], (d, peer))

    def g_col_wait(step):
        slot = (c + step) % 8
        remote(g_send.at[slot], g_recv.at[slot], gcol_s.at[0], gcol_r.at[slot], sibling).wait_recv()

    def g_dp(step):
        return remote(g_all.at[q], g_all.at[q], gdp_s.at[step], gdp_r.at[q], (((q + step) % 8) * 2 + k, c))

    def g_dp_wait(step):
        slot = (q + step) % 8
        remote(g_all.at[slot], g_all.at[slot], gdp_s.at[0], gdp_r.at[slot], sibling).wait_recv()

    send_left = remote(l_send.at[:, pl.ds(512, 512)], l_recv, sib_s.at[10], sib_r.at[10], sibling)

    def g_start():
        for mat in range(2):
            g_send[:, 64 * mat:64 * mat + 64] = g_acc[mat].astype(BF).reshape(8, 64, 128)
        for step in range(1, 8):
            g_col(step).start()

    def g_share():
        total = f32(g_send[c])
        for step in range(1, 8):
            g_col_wait(step)
            total = total + f32(g_recv[(c + step) % 8])
        g_all[q] = total.astype(BF)
        for step in range(1, 8):
            g_dp(step).start()

    def left_products():
        for step in range(1, 8):
            g_dp_wait(step)
        g = jnp.concatenate([g_all[n] for n in range(8)], axis=1)
        for h in range(2):
            cols = slice(512 * h, 512 * h + 512)
            l_send[:, cols] = dot(g, tok[:, :, cols].reshape(1024, 512))
        send_left.start()

    def left_final():
        send_left.wait_recv()
        total = adapter_scale * (l_send[:, 0:512] + l_recv[...])
        gate_lg[...] = total[0:64]
        up_lg[...] = total[64:128]

    pass_on(0)
    for copy in direct(1):
        copy.start()
    pl.loop(0, 3)(merge)
    pass_far(0)
    pl.loop(3, NJ)(merge)
    own_tokens.wait()
    wait_rest(0)

    @pl.loop(0, 2)
    def _(j):
        send_weights(j).wait_recv()
        products(j, 0)
        gate_sum.step1(j, 0)
        up_sum.step1(j, 0)

    pass_on(1)

    @pl.loop(2, NJ)
    def _(j):
        send_weights(j).wait_recv()
        products(j, 0)
        gate_sum.step1(j, 0)

    pass_far(1)
    up_sum.step1(2, 0)
    send_low_w.wait_recv()
    wait_rest(1)
    low_start()
    load_hgrad.wait()
    g_acc[...] = jnp.zeros_like(g_acc)

    @pl.loop(0, NJ + 7)
    def _(i):
        def lag(n, *stages):
            @pl.when((i >= n) & (i < n + NJ))
            def _():
                for stage in stages:
                    stage(i - n)

        def once(n, stage):
            @pl.when(i == n)
            def _():
                stage()

        lag(0, rest_of_products)
        once(0, lambda: low_sum.step2(0))
        lag(1, gate_sum.step2, up_sum.step2)
        once(1, lambda: low_sum.step3(0))
        lag(2, gate_sum.step3, up_sum.step3)
        once(2, low_share)
        lag(3, activate)
        once(3, low_swap)
        once(4, low_pick)
        once(9, g_start)
        lag(4, right_products)
        lag(5, right_sum.step2)
        once(10, g_share)
        lag(6, right_sum.step3)
        once(11, left_products)
        lag(7, right_final)
        once(12, left_final)

    @pl.loop(0, NJ)
    def _(j):
        for total in (gate_sum, up_sum, right_sum):
            total.drain(j)
        send_weights(j).wait_send()
        send_delta(j).wait_send()

    low_sum.drain(0)
    send_low_w.wait_send()
    send_low_sel.wait_send()
    send_left.wait_send()
    for h in range(2):
        for copy in direct(h) + passed(h):
            copy.wait_send()
    for step in range(1, 8):
        low_copy(step).wait_send()
        g_col(step).wait_send()
        g_dp(step).wait_send()


def write_out(*refs):
    sems = refs[-1]
    copies = [pltpu.make_async_copy(refs[n], refs[7 + n], sems.at[n]) for n in range(7)]
    for copy in copies:
        copy.start()
    for copy in copies:
        copy.wait()


def local(*args):
    hbm = pl.BlockSpec(memory_space=pl.ANY)
    vmem = pl.BlockSpec(memory_space=pltpu.VMEM)

    def bf(*shape):
        return pltpu.VMEM(shape, BF)

    def fl(*shape):
        return pltpu.VMEM(shape, F32)

    def dma(*shape):
        return pltpu.SemaphoreType.DMA(shape)

    def x_first(n, rows, width):
        return [bf(n, 4, 2, rows, width), bf(n, 2, rows, width), bf(n, 2, 2, rows, width), bf(n, rows, width)]

    def z_first(n, rows, width):
        return [bf(n, 4, 2, rows, width), bf(n, 4, rows, width), bf(n, 2, rows // 2, width), bf(n, 2, rows, width)]

    scratch = [
        bf(8, 128, 1024), bf(NJ, 1024, 2 * CW), bf(NJ, 2, 512, CW), bf(NJ, 2, 512, CW), bf(NJ, 2, 512, CW),
        bf(4, 512, 512), bf(1024, 128), bf(128, NJ * CW),
        *x_first(NJ, 128, CW), *z_first(NJ, 128, CW),
        *x_first(1, 128, 128),
        *x_first(NJ, 64, CW),
        bf(NJ, 2, 2, 128, CW), bf(8, 2, 2, 32, 128), bf(8, 2, 32, 128), bf(2, 256, 256),
        fl(2, 512, 128), bf(8, 128, 128), bf(8, 128, 128), bf(8, 128, 128), fl(128, 512), fl(128, 1024),
        dma(NJ, 6), dma(6), dma(11), dma(11), dma(24), dma(8, 2, 2),
        dma(NJ, 11), dma(NJ, 11), dma(NJ, 8), dma(NJ, 8), dma(1, 7), dma(1, 7),
        dma(NJ, 7), dma(NJ, 7),
        dma(NJ), dma(NJ), dma(8), dma(8), dma(8), dma(8), dma(8), dma(8),
    ]
    shapes = [((512, 1792), BF)] * 2 + [((128, 1792), BF)] + [((32, 1792), F32)] * 2 + [((64, 512), F32)] * 2
    held = pl.pallas_call(
        kernel,
        out_shape=tuple(pltpu.VMEM(shape, dtype) for shape, dtype in shapes),
        in_specs=[hbm] * 12,
        out_specs=(vmem,) * 7,
        scratch_shapes=scratch,
        compiler_params=pltpu.CompilerParams(
            collective_id=0, has_side_effects=True, vmem_limit_bytes=VMEM_LIMIT
        ),
        cost_estimate=pl.CostEstimate(flops=14_000_000_000, bytes_accessed=24_000_000, transcendentals=230_000),
    )(*args)
    outs = pl.pallas_call(
        write_out,
        out_shape=tuple(jax.ShapeDtypeStruct(shape, dtype) for shape, dtype in shapes),
        in_specs=[vmem] * 7,
        out_specs=(hbm,) * 7,
        scratch_shapes=[dma(7)],
        compiler_params=pltpu.CompilerParams(has_side_effects=True, vmem_limit_bytes=1024 * 1024),
    )(*held)
    return *outs[:5], outs[5].T, outs[6].T


def solution(mesh):
    rows, cols = P("dp", None), P(None, "col")
    both = P("dp", "col")
    return jax.shard_map(
        local,
        mesh=mesh,
        in_specs=(P("col", "dp"), both, both, rows, cols, rows, cols, rows, cols, rows, cols, both),
        out_specs=(both,) * 7,
        check_vma=False,
    )
```

```python
import jax
import jax.numpy as jnp
from jax import lax
from jax.experimental import pallas as pl
from jax.experimental.pallas import tpu as pltpu
from jax.sharding import PartitionSpec as P

adapter_scale = 0.5
MESH = pl.DeviceIdType.MESH
NJ = 7
CW = 256
UX = 16
XR, ZR = 64 + UX, 64 - UX
BF = jnp.bfloat16
F32 = jnp.float32
VMEM_LIMIT = 54 * 1024 * 1024


def f32(value):
    return value.astype(F32)


def dot(left, right, dims=((1,), (0,))):
    return lax.dot_general(left, right, (dims, ((), ())), preferred_element_type=F32)


def kernel(
    tokens, gate_w, up_w, gate_b_old, gate_a_old, up_b_old, up_a_old,
    gate_b_new, gate_right, up_b_new, up_right, hidden_grad,
    merged_gate, merged_up, hidden, gate_rg, up_rg, gate_lg, up_lg,
    tok, wts, raw, a_old, right, fac, low_w, hgrad,
    gp, gxo, gxn, gz, up, uz, uxo, uxn,
    lp, lz, lxo, lxn,
    rp, rxo, rxn, rz,
    delta, low_t, low_sib, low_sel,
    g_acc, g_send, g_recv, g_all, l_recv, l_send,
    in_sem, tok_in_sem, sib_s, sib_r, ag_s, ag_r,
    gp_s, gp_r, up_s, up_r, lp_s, lp_r, rp_s, rp_r,
    dl_s, dl_r, col_s, col_r, gcol_s, gcol_r, gdp_s, gdp_r,
):
    d = lax.axis_index("dp")
    c = lax.axis_index("col")
    q, k = d // 2, d % 2
    x, z = q // 2, q % 2
    zh, y = c // 4, c % 4
    xr, xl, xo = (x + 1) % 4, (x + 3) % 4, (x + 2) % 4
    yr, yl, yo = (y + 1) % 4, (y + 3) % 4, (y + 2) % 4

    def at_chip(xx, zz):
        return ((xx * 2 + zz) * 2 + k, c)

    def at_col(hh, yy):
        return (d, hh * 4 + yy)

    sibling = (q * 2 + 1 - k, c)
    to_right, to_left, to_z = at_chip(xr, z), at_chip(xl, z), at_chip(x, 1 - z)

    def remote(src, dst, send, recv, device):
        return pltpu.make_async_remote_copy(
            src_ref=src, dst_ref=dst, send_sem=send, recv_sem=recv,
            device_id=device, device_id_type=MESH,
        )

    weights = (gate_w, up_w, gate_a_old, up_a_old, gate_right, up_right)

    def load(n, j):
        held = (raw, raw, a_old, a_old, right, right)[n]
        cols = pl.ds(pl.multiple_of(j * CW, CW), CW)
        return pltpu.make_async_copy(weights[n].at[:, cols], held.at[j, n % 2], in_sem.at[j, n])

    factors = (gate_b_old, up_b_old, gate_b_new, up_b_new)

    def load_factor(n):
        return pltpu.make_async_copy(factors[n], fac.at[n], tok_in_sem.at[n])

    own_tokens = pltpu.make_async_copy(
        tokens.at[pl.ds(pl.multiple_of(k * 128, 128), 128)],
        tok.at[c, :, pl.ds(0, 512)], tok_in_sem.at[4],
    )
    load_hgrad = pltpu.make_async_copy(hidden_grad, hgrad, tok_in_sem.at[5])
    barrier = pltpu.get_barrier_semaphore()

    def greet(device):
        pl.semaphore_signal(barrier, inc=1, device_id=device, device_id_type=MESH)

    to_yr, to_yl, to_zo = at_col(zh, yr), at_col(zh, yl), at_col(1 - zh, y)
    greet(sibling)
    for there in (to_yr, to_yl, to_zo):
        greet((q * 2 + 1 - k, there[1]))
    for step in range(1, 8):
        greet((((q + step) % 8) * 2 + k, c))
        greet((d, (c + step) % 8))
    own_tokens.start()
    pl.semaphore_wait(barrier, 18)

    own, other = zh * 4, (1 - zh) * 4

    def rows_of(core, h):
        return tokens.at[pl.ds(pl.multiple_of(core * 128 + 64 * h, 64), 64)]

    def own_width(n, device, h, slot=c):
        dst = tok.at[slot, pl.ds(64 * h, 64), pl.ds(0, 512)]
        return remote(rows_of(k, h), dst, ag_s.at[12 * h + n], ag_r.at[slot, h, 0], device)

    def sib_width(n, device, h, slot=c):
        dst = tok.at[slot, pl.ds(64 * h, 64), pl.ds(512, 512)]
        there = (q * 2 + 1 - k, device[1])
        return remote(rows_of(1 - k, h), dst, ag_s.at[12 * h + n], ag_r.at[slot, h, 1], there)

    def block(n, slot, h, part, device):
        ref = tok.at[slot, pl.ds(64 * h, 64) if part is None else pl.ds(64 * h + 32 * part, 32)]
        return remote(ref, ref, ag_s.at[12 * h + n], ag_r.at[slot, h, part or 0], device)

    def direct(h):
        return (
            own_width(0, to_yr, h), own_width(1, to_yl, h), sib_width(2, to_yr, h), sib_width(3, to_yl, h),
            own_width(4, to_zo, h), sib_width(5, to_zo, h), sib_width(6, (d, c), h),
        )

    def passed(h):
        return (
            block(7, own + yl, h, 0, to_yr), block(8, own + yr, h, 1, to_yl),
            block(9, other + y, h, None, to_yr), block(10, other + y, h, None, to_yl),
            block(11, own + yo, h, None, to_zo),
        )

    def wait_direct(slot, h):
        own_width(0, to_yr, h, slot).wait_recv()
        sib_width(0, to_yr, h, slot).wait_recv()

    def pass_on(h):
        copies = passed(h)
        wait_direct(own + yl, h)
        copies[0].start()
        wait_direct(own + yr, h)
        copies[1].start()
        wait_direct(other + y, h)
        copies[2].start()
        copies[3].start()

    def pass_far(h):
        for part in range(2):
            block(0, own + yo, h, part, to_yr).wait_recv()
        passed(h)[4].start()

    def wait_rest(h):
        sib_width(0, to_yr, h).wait_recv()
        for slot in (other + yl, other + yr, other + yo):
            block(0, slot, h, None, to_yr).wait_recv()

    for copy in direct(0):
        copy.start()
    for n in range(4):
        load_factor(n).start()

    @pl.loop(0, NJ)
    def _(j):
        for n in range(6):
            load(n, j).start()

    load_hgrad.start()

    def send_weights(j):
        return remote(wts.at[j, pl.ds(0, 512)], wts.at[j, pl.ds(512, 512)], sib_s.at[2 + j], sib_r.at[2 + j], sibling)

    def merge(j):
        cols = pl.ds(pl.multiple_of(j * CW, CW), CW)
        for n in range(6):
            load(n, j).wait()
        for mat in range(2):
            merged = f32(raw[j, mat]) + adapter_scale * dot(fac[mat], a_old[j, mat])
            merged = merged.astype(BF)
            (merged_gate, merged_up)[mat][:, cols] = merged
            folded = f32(merged) + adapter_scale * dot(fac[2 + mat], right[j, mat])
            wts[j, 0:512, mat * CW:(mat + 1) * CW] = folded.astype(BF)
        send_weights(j).start()

    for n in range(4):
        load_factor(n).wait()
    low_cols = pl.ds(pl.multiple_of((c % 4) * 128, 128), 128)
    low_w[0:512, :] = jnp.where(c < 4, fac[2, :, low_cols], fac[3, :, low_cols])
    send_low_w = remote(low_w.at[pl.ds(0, 512)], low_w.at[pl.ds(512, 512)], sib_s.at[1], sib_r.at[1], sibling)
    send_low_w.start()

    class Sum:
        def parts(self, n):
            return (0, 1) if self.halves and n in self.first_copies else (None,)

        def copy(self, j, n, h=None):
            src, dst, device = self.pairs(j, slice(None) if h is None else pl.ds(self.half * h, self.half))[n]
            sem = n + 7 if h == 1 else n
            return remote(src, dst, self.send.at[j, sem], self.recv.at[j, sem], device)

        def step1(self, j, h=None):
            for n in self.first_copies:
                self.copy(j, n, h).start()

        def wait(self, j, n):
            for h in self.parts(n):
                self.copy(j, n, h).wait_recv()

        def drain(self, j):
            for n in range(7):
                for h in self.parts(n):
                    self.copy(j, n, h).wait_send()

    class XFirst(Sum):
        first_copies = (0, 1, 2, 3)

        def __init__(self, part, opp, near, last, send, recv, halves=False):
            self.part, self.opp, self.near, self.last = part, opp, near, last
            self.half = part.shape[3] // 2
            self.send, self.recv, self.halves = send, recv, halves

        def pairs(self, j, rows):
            part, opp, near = self.part, self.opp, self.near
            return (
                (part.at[j, xo, 0, rows], opp.at[j, 0, rows], to_right),
                (part.at[j, xo, 1, rows], opp.at[j, 1, rows], to_left),
                (part.at[j, xr, 1, rows], near.at[j, 0, 1, rows], to_right),
                (part.at[j, xl, 0, rows], near.at[j, 1, 0, rows], to_left),
                (part.at[j, xr, 0], near.at[j, 0, 0], to_right),
                (part.at[j, xl, 1], near.at[j, 1, 1], to_left),
                (part.at[j, x, 1 - z], self.last.at[j], to_z),
            )

        def step2(self, j):
            part = self.part
            self.wait(j, 0)
            part[j, xr, 0] = (f32(part[j, xr, 0]) + f32(self.opp[j, 0])).astype(BF)
            self.copy(j, 4).start()
            self.wait(j, 1)
            part[j, xl, 1] = (f32(part[j, xl, 1]) + f32(self.opp[j, 1])).astype(BF)
            self.copy(j, 5).start()

        def step3(self, j):
            for n in range(2, 6):
                self.wait(j, n)
            near = self.near
            self.part[j, x, 1 - z] = (
                f32(self.part[j, x, 1 - z]) + f32(near[j, 0, 1 - z]) + f32(near[j, 1, 1 - z])
            ).astype(BF)
            self.copy(j, 6).start()

        def final(self, j):
            self.wait(j, 6)
            near = self.near
            return f32(self.part[j, x, z]) + f32(near[j, 0, z]) + f32(near[j, 1, z]) + f32(self.last[j])

    class ZFirst(Sum):
        first_copies = (0,)

        def __init__(self, part, first, opp, near, send, recv, halves=False):
            self.part, self.first, self.opp, self.near = part, first, opp, near
            self.send, self.recv, self.halves = send, recv, halves
            self.half = self.rows = part.shape[3] // 2

        def pairs(self, j, rows):
            low, high = pl.ds(0, self.rows), pl.ds(self.rows, self.rows)
            part, opp, near = self.part, self.opp, self.near
            return (
                (part.at[j, :, 1 - z, rows], self.first.at[j, :, rows], to_z),
                (part.at[j, xo, z, low], opp.at[j, 0], to_right),
                (part.at[j, xo, z, high], opp.at[j, 1], to_left),
                (part.at[j, xr, z, high], near.at[j, 0, high], to_right),
                (part.at[j, xl, z, low], near.at[j, 1, low], to_left),
                (part.at[j, xr, z, low], near.at[j, 0, low], to_right),
                (part.at[j, xl, z, high], near.at[j, 1, high], to_left),
            )

        def step2(self, j):
            self.wait(j, 0)
            part = self.part
            for xx in (xo, xr, xl, x):
                part[j, xx, z] = (f32(part[j, xx, z]) + f32(self.first[j, xx])).astype(BF)
            for n in range(1, 5):
                self.copy(j, n).start()

        def step3(self, j):
            part, n = self.part, self.rows
            self.wait(j, 1)
            part[j, xr, z, 0:n] = (f32(part[j, xr, z, 0:n]) + f32(self.opp[j, 0])).astype(BF)
            self.copy(j, 5).start()
            self.wait(j, 2)
            part[j, xl, z, n:2 * n] = (f32(part[j, xl, z, n:2 * n]) + f32(self.opp[j, 1])).astype(BF)
            self.copy(j, 6).start()

        def final(self, j):
            for n in range(3, 7):
                self.wait(j, n)
            return f32(self.part[j, x, z]) + f32(self.near[j, 0]) + f32(self.near[j, 1])

    gate_sum = XFirst(gp, gxo, gxn, gz, gp_s, gp_r, halves=True)
    up_sum = ZFirst(up, uz, uxo, uxn, up_s, up_r, halves=True)
    low_sum = ZFirst(lp, lz, lxo, lxn, lp_s, lp_r)
    right_sum = XFirst(rp, rxo, rxn, rz, rp_s, rp_r)

    def low_copy(step):
        return remote(low_t.at[c], low_t.at[c], col_s.at[step], col_r.at[c], (d, (c + step) % 8))

    def low_wait(step):
        slot = (c + step) % 8
        remote(low_t.at[slot], low_t.at[slot], col_s.at[0], col_r.at[slot], sibling).wait_recv()

    send_low_sel = remote(low_t.at[:, :, 1 - k], low_sib, sib_s.at[9], sib_r.at[9], sibling)

    def low_start():
        for h in range(2):
            rows = tok[4 * h:4 * h + 4].reshape(512, 1024)
            lp[0, 2 * h:2 * h + 2] = dot(rows, low_w[...]).astype(BF).reshape(2, 2, 128, 128)
        low_sum.step1(0)

    def low_share():
        low_t[c] = low_sum.final(0).T.astype(BF).reshape(2, 2, 32, 128)
        for step in range(1, 8):
            low_copy(step).start()

    def low_swap():
        for step in range(1, 8):
            low_wait(step)
        send_low_sel.start()

    def low_pick():
        send_low_sel.wait_recv()
        for mat in range(2):
            low_sel[mat, :, 0:128] = low_t[4 * mat:4 * mat + 4, :, k].reshape(256, 128)
            low_sel[mat, :, 128:256] = low_sib[4 * mat:4 * mat + 4].reshape(256, 128)

    def products(j, h):
        part = slice(64 * h, 64 * h + 64)
        terms = dot(tok[:, part].reshape(512, 1024), wts[j]).astype(BF)
        terms = terms.reshape(4, 2, 64, 2 * CW)
        gp[j, :, :, XR * h:XR * h + 64] = terms[..., 0:CW]
        gp[j, :, :, XR * h + 64:XR * h + XR] = terms[:, :, 0:UX, CW:2 * CW]
        up[j, :, :, ZR * h:ZR * h + ZR] = terms[:, :, UX:64, CW:2 * CW]

    def rest_of_products(j):
        products(j, 1)
        gate_sum.step1(j, 1)
        up_sum.step1(j, 1)

        @pl.when(j > 2)
        def _():
            up_sum.step1(j, 0)

    def send_delta(j):
        return remote(delta.at[j, :, 0], delta.at[j, :, 1], dl_s.at[j], dl_r.at[j], sibling)

    def activate(j):
        cols = pl.ds(pl.multiple_of(j * CW, CW), CW)
        xs = gate_sum.final(j)
        zs = up_sum.final(j)
        gate = jnp.concatenate([xs[0:64], xs[XR:XR + 64]])
        upv = jnp.concatenate([xs[64:XR], zs[0:ZR], xs[XR + 64:2 * XR], zs[ZR:2 * ZR]])
        sg = 1.0 / (1.0 + jnp.exp(-gate))
        active = gate * sg
        hidden[:, cols] = (active * upv).astype(BF)
        upstream = f32(hgrad[:, cols])
        delta[j, 0, 0] = (upstream * upv * sg * (1.0 + gate * (1.0 - sg))).astype(BF)
        delta[j, 1, 0] = (upstream * active).astype(BF)
        send_delta(j).start()
        for mat in range(2):
            g_acc[mat] += dot(right[j, mat], delta[j, mat, 0], ((1,), (1,)))

    def right_products(j):
        send_delta(j).wait_recv()
        for mat in range(2):
            terms = dot(low_sel[mat], delta[j, mat].reshape(256, CW)).astype(BF)
            rp[j, :, :, 32 * mat:32 * mat + 32] = terms.reshape(4, 2, 32, CW)
        right_sum.step1(j)

    def right_final(j):
        cols = pl.ds(pl.multiple_of(j * CW, CW), CW)
        total = adapter_scale * right_sum.final(j)
        gate_rg[:, cols] = total[0:32]
        up_rg[:, cols] = total[32:64]

    def g_col(step):
        peer = (c + step) % 8
        return remote(g_send.at[peer], g_recv.at[c], gcol_s.at[step], gcol_r.at[c], (d, peer))

    def g_col_wait(step):
        slot = (c + step) % 8
        remote(g_send.at[slot], g_recv.at[slot], gcol_s.at[0], gcol_r.at[slot], sibling).wait_recv()

    def g_dp(step):
        return remote(g_all.at[q], g_all.at[q], gdp_s.at[step], gdp_r.at[q], (((q + step) % 8) * 2 + k, c))

    def g_dp_wait(step):
        slot = (q + step) % 8
        remote(g_all.at[slot], g_all.at[slot], gdp_s.at[0], gdp_r.at[slot], sibling).wait_recv()

    send_left = remote(l_send.at[:, pl.ds(512, 512)], l_recv, sib_s.at[10], sib_r.at[10], sibling)

    def g_start():
        for mat in range(2):
            g_send[:, 64 * mat:64 * mat + 64] = g_acc[mat].astype(BF).reshape(8, 64, 128)
        for step in range(1, 8):
            g_col(step).start()

    def g_share():
        total = f32(g_send[c])
        for step in range(1, 8):
            g_col_wait(step)
            total = total + f32(g_recv[(c + step) % 8])
        g_all[q] = total.astype(BF)
        for step in range(1, 8):
            g_dp(step).start()

    def left_products():
        for step in range(1, 8):
            g_dp_wait(step)
        g = jnp.concatenate([g_all[n] for n in range(8)], axis=1)
        for h in range(2):
            cols = slice(512 * h, 512 * h + 512)
            l_send[:, cols] = dot(g, tok[:, :, cols].reshape(1024, 512))
        send_left.start()

    def left_final():
        send_left.wait_recv()
        total = adapter_scale * (l_send[:, 0:512] + l_recv[...])
        gate_lg[...] = total[0:64]
        up_lg[...] = total[64:128]

    pass_on(0)
    for copy in direct(1):
        copy.start()
    pl.loop(0, 3)(merge)
    pass_far(0)
    pl.loop(3, NJ)(merge)
    own_tokens.wait()
    wait_rest(0)

    @pl.loop(0, 2)
    def _(j):
        send_weights(j).wait_recv()
        products(j, 0)
        gate_sum.step1(j, 0)
        up_sum.step1(j, 0)

    pass_on(1)

    @pl.loop(2, NJ)
    def _(j):
        send_weights(j).wait_recv()
        products(j, 0)
        gate_sum.step1(j, 0)

    pass_far(1)
    up_sum.step1(2, 0)
    send_low_w.wait_recv()
    wait_rest(1)
    low_start()
    load_hgrad.wait()
    g_acc[...] = jnp.zeros_like(g_acc)

    @pl.loop(0, NJ + 7)
    def _(i):
        def lag(n, *stages):
            @pl.when((i >= n) & (i < n + NJ))
            def _():
                for stage in stages:
                    stage(i - n)

        def early(n, stage):
            @pl.when((i >= n) & (i < n + 5))
            def _():
                stage(i - n)

        def late(n, stage):
            @pl.when(i == n)
            def _():
                pl.loop(5, NJ)(stage)

        def once(n, stage):
            @pl.when(i == n)
            def _():
                stage()

        lag(0, rest_of_products)
        once(0, lambda: low_sum.step2(0))
        lag(1, gate_sum.step2, up_sum.step2)
        once(1, lambda: low_sum.step3(0))
        lag(2, gate_sum.step3, up_sum.step3)
        once(2, low_share)
        lag(3, activate)
        once(NJ + 2, g_start)
        once(3, low_swap)
        once(4, low_pick)
        early(5, right_products)
        late(NJ + 3, right_products)
        early(5+1, right_sum.step2)
        late(NJ + 4, right_sum.step2)
        once(NJ + 3, g_share)
        early(5+2, right_sum.step3)
        late(NJ + 5, right_sum.step3)
        once(NJ + 4, left_products)
        early(5+3, right_final)
        once(NJ + 5, left_final)
        late(NJ + 6, right_final)

    @pl.loop(0, NJ)
    def _(j):
        for total in (gate_sum, up_sum, right_sum):
            total.drain(j)
        send_weights(j).wait_send()
        send_delta(j).wait_send()

    low_sum.drain(0)
    send_low_w.wait_send()
    send_low_sel.wait_send()
    send_left.wait_send()
    for h in range(2):
        for copy in direct(h) + passed(h):
            copy.wait_send()
    for step in range(1, 8):
        low_copy(step).wait_send()
        g_col(step).wait_send()
        g_dp(step).wait_send()


def write_out(*refs):
    sems = refs[-1]
    copies = [pltpu.make_async_copy(refs[n], refs[7 + n], sems.at[n]) for n in range(7)]
    for copy in copies:
        copy.start()
    for copy in copies:
        copy.wait()


def local(*args):
    hbm = pl.BlockSpec(memory_space=pl.ANY)
    vmem = pl.BlockSpec(memory_space=pltpu.VMEM)

    def bf(*shape):
        return pltpu.VMEM(shape, BF)

    def fl(*shape):
        return pltpu.VMEM(shape, F32)

    def dma(*shape):
        return pltpu.SemaphoreType.DMA(shape)

    def x_first(n, rows, width):
        return [bf(n, 4, 2, rows, width), bf(n, 2, rows, width), bf(n, 2, 2, rows, width), bf(n, rows, width)]

    def z_first(n, rows, width):
        return [bf(n, 4, 2, rows, width), bf(n, 4, rows, width), bf(n, 2, rows // 2, width), bf(n, 2, rows, width)]

    scratch = [
        bf(8, 128, 1024), bf(NJ, 1024, 2 * CW), bf(NJ, 2, 512, CW), bf(NJ, 2, 512, CW), bf(NJ, 2, 512, CW),
        bf(4, 512, 512), bf(1024, 128), bf(128, NJ * CW),
        *x_first(NJ, 2 * XR, CW), *z_first(NJ, 2 * ZR, CW),
        *z_first(1, 128, 128),
        *x_first(NJ, 64, CW),
        bf(NJ, 2, 2, 128, CW), bf(8, 2, 2, 32, 128), bf(8, 2, 32, 128), bf(2, 256, 256),
        fl(2, 512, 128), bf(8, 128, 128), bf(8, 128, 128), bf(8, 128, 128), fl(128, 512), fl(128, 1024),
        dma(NJ, 6), dma(6), dma(11), dma(11), dma(24), dma(8, 2, 2),
        dma(NJ, 11), dma(NJ, 11), dma(NJ, 8), dma(NJ, 8), dma(1, 7), dma(1, 7),
        dma(NJ, 7), dma(NJ, 7),
        dma(NJ), dma(NJ), dma(8), dma(8), dma(8), dma(8), dma(8), dma(8),
    ]
    shapes = [((512, 1792), BF)] * 2 + [((128, 1792), BF)] + [((32, 1792), F32)] * 2 + [((64, 512), F32)] * 2
    held = pl.pallas_call(
        kernel,
        out_shape=tuple(pltpu.VMEM(shape, dtype) for shape, dtype in shapes),
        in_specs=[hbm] * 12,
        out_specs=(vmem,) * 7,
        scratch_shapes=scratch,
        compiler_params=pltpu.CompilerParams(
            collective_id=0, has_side_effects=True, vmem_limit_bytes=VMEM_LIMIT
        ),
        cost_estimate=pl.CostEstimate(flops=14_000_000_000, bytes_accessed=24_000_000, transcendentals=230_000),
    )(*args)
    outs = pl.pallas_call(
        write_out,
        out_shape=tuple(jax.ShapeDtypeStruct(shape, dtype) for shape, dtype in shapes),
        in_specs=[vmem] * 7,
        out_specs=(hbm,) * 7,
        scratch_shapes=[dma(7)],
        compiler_params=pltpu.CompilerParams(has_side_effects=True, vmem_limit_bytes=1024 * 1024),
    )(*held)
    return *outs[:5], outs[5].T, outs[6].T


def solution(mesh):
    rows, cols = P("dp", None), P(None, "col")
    both = P("dp", "col")
    return jax.shard_map(
        local,
        mesh=mesh,
        in_specs=(P("col", "dp"), both, both, rows, cols, rows, cols, rows, cols, rows, cols, both),
        out_specs=(both,) * 7,
        check_vma=False,
    )
```

```python
import jax
import jax.numpy as jnp
from jax import lax
from jax.experimental import pallas as pl
from jax.experimental.pallas import tpu as pltpu
from jax.sharding import PartitionSpec as P

adapter_scale = 0.5
MESH = pl.DeviceIdType.MESH
NJ = 7
CW = 256
UX = 16
XR, ZR = 64 + UX, 64 - UX
BF = jnp.bfloat16
F32 = jnp.float32
VMEM_LIMIT = 54 * 1024 * 1024


def f32(value):
    return value.astype(F32)


def dot(left, right, dims=((1,), (0,))):
    return lax.dot_general(left, right, (dims, ((), ())), preferred_element_type=F32)


def kernel(
    tokens, gate_w, up_w, gate_b_old, gate_a_old, up_b_old, up_a_old,
    gate_b_new, gate_right, up_b_new, up_right, hidden_grad,
    merged_gate, merged_up, hidden, gate_rg, up_rg, gate_lg, up_lg,
    tok, wts, raw, a_old, right, fac, low_w, hgrad,
    gp, gxo, gxn, gz, up, uz, uxo, uxn,
    lp, lz, lxo, lxn,
    rp, rxo, rxn, rz,
    delta, low_t, low_sib, low_sel,
    g_acc, g_send, g_recv, g_all, l_recv, l_send,
    in_sem, tok_in_sem, sib_s, sib_r, ag_s, ag_r,
    gp_s, gp_r, up_s, up_r, lp_s, lp_r, rp_s, rp_r,
    dl_s, dl_r, col_s, col_r, gcol_s, gcol_r, gdp_s, gdp_r,
):
    d = lax.axis_index("dp")
    c = lax.axis_index("col")
    q, k = d // 2, d % 2
    x, z = q // 2, q % 2
    zh, y = c // 4, c % 4
    xr, xl, xo = (x + 1) % 4, (x + 3) % 4, (x + 2) % 4
    yr, yl, yo = (y + 1) % 4, (y + 3) % 4, (y + 2) % 4

    def at_chip(xx, zz):
        return ((xx * 2 + zz) * 2 + k, c)

    def at_col(hh, yy):
        return (d, hh * 4 + yy)

    sibling = (q * 2 + 1 - k, c)
    to_right, to_left, to_z = at_chip(xr, z), at_chip(xl, z), at_chip(x, 1 - z)

    def remote(src, dst, send, recv, device):
        return pltpu.make_async_remote_copy(
            src_ref=src, dst_ref=dst, send_sem=send, recv_sem=recv,
            device_id=device, device_id_type=MESH,
        )

    weights = (gate_w, up_w, gate_a_old, up_a_old, gate_right, up_right)

    def load(n, j):
        held = (raw, raw, a_old, a_old, right, right)[n]
        cols = pl.ds(pl.multiple_of(j * CW, CW), CW)
        return pltpu.make_async_copy(weights[n].at[:, cols], held.at[j, n % 2], in_sem.at[j, n])

    factors = (gate_b_old, up_b_old, gate_b_new, up_b_new)

    def load_factor(n):
        return pltpu.make_async_copy(factors[n], fac.at[n], tok_in_sem.at[n])

    own_tokens = pltpu.make_async_copy(
        tokens.at[pl.ds(pl.multiple_of(k * 128, 128), 128)],
        tok.at[c, :, pl.ds(0, 512)], tok_in_sem.at[4],
    )
    load_hgrad = pltpu.make_async_copy(hidden_grad, hgrad, tok_in_sem.at[5])
    barrier = pltpu.get_barrier_semaphore()

    def greet(device):
        pl.semaphore_signal(barrier, inc=1, device_id=device, device_id_type=MESH)

    to_yr, to_yl, to_zo = at_col(zh, yr), at_col(zh, yl), at_col(1 - zh, y)
    greet(sibling)
    for there in (to_yr, to_yl, to_zo):
        greet((q * 2 + 1 - k, there[1]))
    for step in range(1, 8):
        greet((((q + step) % 8) * 2 + k, c))
        greet((d, (c + step) % 8))
    own_tokens.start()
    pl.semaphore_wait(barrier, 18)

    own, other = zh * 4, (1 - zh) * 4

    def rows_of(core, h):
        return tokens.at[pl.ds(pl.multiple_of(core * 128 + 64 * h, 64), 64)]

    def own_width(n, device, h, slot=c):
        dst = tok.at[slot, pl.ds(64 * h, 64), pl.ds(0, 512)]
        return remote(rows_of(k, h), dst, ag_s.at[12 * h + n], ag_r.at[slot, h, 0], device)

    def sib_width(n, device, h, slot=c):
        dst = tok.at[slot, pl.ds(64 * h, 64), pl.ds(512, 512)]
        there = (q * 2 + 1 - k, device[1])
        return remote(rows_of(1 - k, h), dst, ag_s.at[12 * h + n], ag_r.at[slot, h, 1], there)

    def block(n, slot, h, part, device):
        ref = tok.at[slot, pl.ds(64 * h, 64) if part is None else pl.ds(64 * h + 32 * part, 32)]
        return remote(ref, ref, ag_s.at[12 * h + n], ag_r.at[slot, h, part or 0], device)

    def direct(h):
        return (
            own_width(0, to_yr, h), own_width(1, to_yl, h), sib_width(2, to_yr, h), sib_width(3, to_yl, h),
            own_width(4, to_zo, h), sib_width(5, to_zo, h), sib_width(6, (d, c), h),
        )

    def passed(h):
        return (
            block(7, own + yl, h, 0, to_yr), block(8, own + yr, h, 1, to_yl),
            block(9, other + y, h, None, to_yr), block(10, other + y, h, None, to_yl),
            block(11, own + yo, h, None, to_zo),
        )

    def wait_direct(slot, h):
        own_width(0, to_yr, h, slot).wait_recv()
        sib_width(0, to_yr, h, slot).wait_recv()

    def pass_on(h):
        copies = passed(h)
        wait_direct(own + yl, h)
        copies[0].start()
        wait_direct(own + yr, h)
        copies[1].start()
        wait_direct(other + y, h)
        copies[2].start()
        copies[3].start()

    def pass_far(h):
        for part in range(2):
            block(0, own + yo, h, part, to_yr).wait_recv()
        passed(h)[4].start()

    def wait_rest(h):
        sib_width(0, to_yr, h).wait_recv()
        for slot in (other + yl, other + yr, other + yo):
            block(0, slot, h, None, to_yr).wait_recv()

    for copy in direct(0):
        copy.start()
    for n in range(4):
        load_factor(n).start()

    @pl.loop(0, NJ)
    def _(j):
        for n in range(6):
            load(n, j).start()

    load_hgrad.start()

    def send_weights(j):
        return remote(wts.at[j, pl.ds(0, 512)], wts.at[j, pl.ds(512, 512)], sib_s.at[2 + j], sib_r.at[2 + j], sibling)

    def merge(j):
        cols = pl.ds(pl.multiple_of(j * CW, CW), CW)
        for n in range(6):
            load(n, j).wait()
        for mat in range(2):
            merged = f32(raw[j, mat]) + adapter_scale * dot(fac[mat], a_old[j, mat])
            merged = merged.astype(BF)
            (merged_gate, merged_up)[mat][:, cols] = merged
            folded = f32(merged) + adapter_scale * dot(fac[2 + mat], right[j, mat])
            wts[j, 0:512, mat * CW:(mat + 1) * CW] = folded.astype(BF)
        send_weights(j).start()

    for n in range(4):
        load_factor(n).wait()
    low_cols = pl.ds(pl.multiple_of((c % 4) * 128, 128), 128)
    low_w[0:512, :] = jnp.where(c < 4, fac[2, :, low_cols], fac[3, :, low_cols])
    send_low_w = remote(low_w.at[pl.ds(0, 512)], low_w.at[pl.ds(512, 512)], sib_s.at[1], sib_r.at[1], sibling)
    send_low_w.start()

    class Sum:
        def parts(self, n):
            return (0, 1) if self.halves and n in self.first_copies else (None,)

        def copy(self, j, n, h=None):
            src, dst, device = self.pairs(j, slice(None) if h is None else pl.ds(self.half * h, self.half))[n]
            sem = n + 7 if h == 1 else n
            return remote(src, dst, self.send.at[j, sem], self.recv.at[j, sem], device)

        def step1(self, j, h=None):
            for n in self.first_copies:
                self.copy(j, n, h).start()

        def wait(self, j, n):
            for h in self.parts(n):
                self.copy(j, n, h).wait_recv()

        def drain(self, j):
            for n in range(7):
                for h in self.parts(n):
                    self.copy(j, n, h).wait_send()

    class XFirst(Sum):
        first_copies = (0, 1, 2, 3)

        def __init__(self, part, opp, near, last, send, recv, halves=False):
            self.part, self.opp, self.near, self.last = part, opp, near, last
            self.half = part.shape[3] // 2
            self.send, self.recv, self.halves = send, recv, halves

        def pairs(self, j, rows):
            part, opp, near = self.part, self.opp, self.near
            return (
                (part.at[j, xo, 0, rows], opp.at[j, 0, rows], to_right),
                (part.at[j, xo, 1, rows], opp.at[j, 1, rows], to_left),
                (part.at[j, xr, 1, rows], near.at[j, 0, 1, rows], to_right),
                (part.at[j, xl, 0, rows], near.at[j, 1, 0, rows], to_left),
                (part.at[j, xr, 0], near.at[j, 0, 0], to_right),
                (part.at[j, xl, 1], near.at[j, 1, 1], to_left),
                (part.at[j, x, 1 - z], self.last.at[j], to_z),
            )

        def step2(self, j):
            part = self.part
            self.wait(j, 0)
            part[j, xr, 0] = (f32(part[j, xr, 0]) + f32(self.opp[j, 0])).astype(BF)
            self.copy(j, 4).start()
            self.wait(j, 1)
            part[j, xl, 1] = (f32(part[j, xl, 1]) + f32(self.opp[j, 1])).astype(BF)
            self.copy(j, 5).start()

        def step3(self, j):
            for n in range(2, 6):
                self.wait(j, n)
            near = self.near
            self.part[j, x, 1 - z] = (
                f32(self.part[j, x, 1 - z]) + f32(near[j, 0, 1 - z]) + f32(near[j, 1, 1 - z])
            ).astype(BF)
            self.copy(j, 6).start()

        def final(self, j):
            self.wait(j, 6)
            near = self.near
            return f32(self.part[j, x, z]) + f32(near[j, 0, z]) + f32(near[j, 1, z]) + f32(self.last[j])

    class ZFirst(Sum):
        first_copies = (0,)

        def __init__(self, part, first, opp, near, send, recv, halves=False):
            self.part, self.first, self.opp, self.near = part, first, opp, near
            self.send, self.recv, self.halves = send, recv, halves
            self.half = self.rows = part.shape[3] // 2

        def pairs(self, j, rows):
            low, high = pl.ds(0, self.rows), pl.ds(self.rows, self.rows)
            part, opp, near = self.part, self.opp, self.near
            return (
                (part.at[j, :, 1 - z, rows], self.first.at[j, :, rows], to_z),
                (part.at[j, xo, z, low], opp.at[j, 0], to_right),
                (part.at[j, xo, z, high], opp.at[j, 1], to_left),
                (part.at[j, xr, z, high], near.at[j, 0, high], to_right),
                (part.at[j, xl, z, low], near.at[j, 1, low], to_left),
                (part.at[j, xr, z, low], near.at[j, 0, low], to_right),
                (part.at[j, xl, z, high], near.at[j, 1, high], to_left),
            )

        def step2(self, j):
            self.wait(j, 0)
            part = self.part
            for xx in (xo, xr, xl, x):
                part[j, xx, z] = (f32(part[j, xx, z]) + f32(self.first[j, xx])).astype(BF)
            for n in range(1, 5):
                self.copy(j, n).start()

        def step3(self, j):
            part, n = self.part, self.rows
            self.wait(j, 1)
            part[j, xr, z, 0:n] = (f32(part[j, xr, z, 0:n]) + f32(self.opp[j, 0])).astype(BF)
            self.copy(j, 5).start()
            self.wait(j, 2)
            part[j, xl, z, n:2 * n] = (f32(part[j, xl, z, n:2 * n]) + f32(self.opp[j, 1])).astype(BF)
            self.copy(j, 6).start()

        def final(self, j):
            for n in range(3, 7):
                self.wait(j, n)
            return f32(self.part[j, x, z]) + f32(self.near[j, 0]) + f32(self.near[j, 1])

    gate_sum = XFirst(gp, gxo, gxn, gz, gp_s, gp_r, halves=True)
    up_sum = ZFirst(up, uz, uxo, uxn, up_s, up_r, halves=True)
    low_sum = ZFirst(lp, lz, lxo, lxn, lp_s, lp_r)
    right_sum = XFirst(rp, rxo, rxn, rz, rp_s, rp_r)

    def low_copy(step):
        return remote(low_t.at[c], low_t.at[c], col_s.at[step], col_r.at[c], (d, (c + step) % 8))

    def low_wait(step):
        slot = (c + step) % 8
        remote(low_t.at[slot], low_t.at[slot], col_s.at[0], col_r.at[slot], sibling).wait_recv()

    send_low_sel = remote(low_t.at[:, :, 1 - k], low_sib, sib_s.at[9], sib_r.at[9], sibling)

    def low_start():
        for h in range(2):
            rows = tok[4 * h:4 * h + 4].reshape(512, 1024)
            lp[0, 2 * h:2 * h + 2] = dot(rows, low_w[...]).astype(BF).reshape(2, 2, 128, 128)
        low_sum.step1(0)

    def low_share():
        low_t[c] = low_sum.final(0).T.astype(BF).reshape(2, 2, 32, 128)
        for step in range(1, 8):
            low_copy(step).start()

    def low_swap():
        for step in range(1, 8):
            low_wait(step)
        send_low_sel.start()

    def low_pick():
        send_low_sel.wait_recv()
        for mat in range(2):
            low_sel[mat, :, 0:128] = low_t[4 * mat:4 * mat + 4, :, k].reshape(256, 128)
            low_sel[mat, :, 128:256] = low_sib[4 * mat:4 * mat + 4].reshape(256, 128)

    def products(j, h):
        part = slice(64 * h, 64 * h + 64)
        terms = dot(tok[:, part].reshape(512, 1024), wts[j]).astype(BF)
        terms = terms.reshape(4, 2, 64, 2 * CW)
        gp[j, :, :, XR * h:XR * h + 64] = terms[..., 0:CW]
        gp[j, :, :, XR * h + 64:XR * h + XR] = terms[:, :, 0:UX, CW:2 * CW]
        up[j, :, :, ZR * h:ZR * h + ZR] = terms[:, :, UX:64, CW:2 * CW]

    def rest_of_products(j):
        products(j, 1)
        gate_sum.step1(j, 1)
        up_sum.step1(j, 1)

        @pl.when(j > 2)
        def _():
            up_sum.step1(j, 0)

    def send_delta(j):
        return remote(delta.at[j, :, 0], delta.at[j, :, 1], dl_s.at[j], dl_r.at[j], sibling)

    def activate(j):
        cols = pl.ds(pl.multiple_of(j * CW, CW), CW)
        xs = gate_sum.final(j)
        zs = up_sum.final(j)
        gate = jnp.concatenate([xs[0:64], xs[XR:XR + 64]])
        upv = jnp.concatenate([xs[64:XR], zs[0:ZR], xs[XR + 64:2 * XR], zs[ZR:2 * ZR]])
        sg = 1.0 / (1.0 + jnp.exp(-gate))
        active = gate * sg
        hidden[:, cols] = (active * upv).astype(BF)
        upstream = f32(hgrad[:, cols])
        delta[j, 0, 0] = (upstream * upv * sg * (1.0 + gate * (1.0 - sg))).astype(BF)
        delta[j, 1, 0] = (upstream * active).astype(BF)
        send_delta(j).start()
        for mat in range(2):
            g_acc[mat] += dot(right[j, mat], delta[j, mat, 0], ((1,), (1,)))

    def right_products(j):
        send_delta(j).wait_recv()
        for mat in range(2):
            terms = dot(low_sel[mat], delta[j, mat].reshape(256, CW)).astype(BF)
            rp[j, :, :, 32 * mat:32 * mat + 32] = terms.reshape(4, 2, 32, CW)
        right_sum.step1(j)

    def right_final(j):
        cols = pl.ds(pl.multiple_of(j * CW, CW), CW)
        total = adapter_scale * right_sum.final(j)
        gate_rg[:, cols] = total[0:32]
        up_rg[:, cols] = total[32:64]

    def g_col(step):
        peer = (c + step) % 8
        return remote(g_send.at[peer], g_recv.at[c], gcol_s.at[step], gcol_r.at[c], (d, peer))

    def g_col_wait(step):
        slot = (c + step) % 8
        remote(g_send.at[slot], g_recv.at[slot], gcol_s.at[0], gcol_r.at[slot], sibling).wait_recv()

    def g_dp(step):
        return remote(g_all.at[q], g_all.at[q], gdp_s.at[step], gdp_r.at[q], (((q + step) % 8) * 2 + k, c))

    def g_dp_wait(step):
        slot = (q + step) % 8
        remote(g_all.at[slot], g_all.at[slot], gdp_s.at[0], gdp_r.at[slot], sibling).wait_recv()

    send_left = remote(l_send.at[:, pl.ds(512, 512)], l_recv, sib_s.at[10], sib_r.at[10], sibling)

    def g_start():
        for mat in range(2):
            g_send[:, 64 * mat:64 * mat + 64] = g_acc[mat].astype(BF).reshape(8, 64, 128)
        for step in range(1, 8):
            g_col(step).start()

    def g_share():
        total = f32(g_send[c])
        for step in range(1, 8):
            g_col_wait(step)
            total = total + f32(g_recv[(c + step) % 8])
        g_all[q] = total.astype(BF)
        for step in range(1, 8):
            g_dp(step).start()

    def left_products():
        for step in range(1, 8):
            g_dp_wait(step)
        g = jnp.concatenate([g_all[n] for n in range(8)], axis=1)
        l_send[:, 512:1024] = dot(g, tok[:, :, 512:1024].reshape(1024, 512))
        send_left.start()
        l_send[:, 0:512] = dot(g, tok[:, :, 0:512].reshape(1024, 512))

    def left_final():
        send_left.wait_recv()
        total = adapter_scale * (l_send[:, 0:512] + l_recv[...])
        gate_lg[...] = total[0:64]
        up_lg[...] = total[64:128]

    pass_on(0)
    for copy in direct(1):
        copy.start()
    pl.loop(0, 3)(merge)
    pass_far(0)
    pl.loop(3, NJ)(merge)
    own_tokens.wait()
    wait_rest(0)

    @pl.loop(0, 2)
    def _(j):
        send_weights(j).wait_recv()
        products(j, 0)
        gate_sum.step1(j, 0)
        up_sum.step1(j, 0)

    pass_on(1)

    @pl.loop(2, NJ)
    def _(j):
        send_weights(j).wait_recv()
        products(j, 0)
        gate_sum.step1(j, 0)

    pass_far(1)
    up_sum.step1(2, 0)
    send_low_w.wait_recv()
    wait_rest(1)
    low_start()
    load_hgrad.wait()
    g_acc[...] = jnp.zeros_like(g_acc)

    @pl.loop(0, NJ + 3)
    def _(i):
        def lag(n, *stages):
            @pl.when((i >= n) & (i < n + NJ))
            def _():
                for stage in stages:
                    stage(i - n)

        def once(n, stage):
            @pl.when(i == n)
            def _():
                stage()

        lag(0, rest_of_products)
        once(0, lambda: low_sum.step2(0))
        lag(1, gate_sum.step2, up_sum.step2)
        once(1, lambda: low_sum.step3(0))
        lag(2, gate_sum.step3, up_sum.step3)
        once(2, low_share)
        lag(3, activate)
        once(NJ + 2, g_start)
        once(3, low_swap)
        once(4, low_pick)
        lag(5, right_products)
        lag(6, right_sum.step2)
        lag(7, right_sum.step3)
        lag(8, right_final)

    @pl.loop(NJ - 2, NJ)
    def _(j):
        right_products(j)

    right_sum.step2(NJ - 3)
    g_share()

    @pl.loop(NJ - 2, NJ)
    def _(j):
        right_sum.step2(j)
        right_sum.step3(j - 2)
        right_final(j - 3)

    right_sum.step3(NJ - 2)
    right_sum.step3(NJ - 1)
    left_products()

    @pl.loop(NJ - 3, NJ)
    def _(j):
        right_final(j)

    left_final()

    @pl.loop(0, NJ)
    def _(j):
        for total in (gate_sum, up_sum, right_sum):
            total.drain(j)
        send_weights(j).wait_send()
        send_delta(j).wait_send()

    low_sum.drain(0)
    send_low_w.wait_send()
    send_low_sel.wait_send()
    send_left.wait_send()
    for h in range(2):
        for copy in direct(h) + passed(h):
            copy.wait_send()
    for step in range(1, 8):
        low_copy(step).wait_send()
        g_col(step).wait_send()
        g_dp(step).wait_send()


def write_out(*refs):
    sems = refs[-1]
    pieces = [(n, pl.ds(128 * m, 128)) for n in range(2) for m in range(4)] + [(n, slice(None)) for n in range(2, 7)]
    copies = [
        pltpu.make_async_copy(refs[n].at[rows], refs[7 + n].at[rows], sems.at[m])
        for m, (n, rows) in enumerate(pieces)
    ]
    for copy in copies:
        copy.start()
    for copy in copies:
        copy.wait()


def local(*args):
    hbm = pl.BlockSpec(memory_space=pl.ANY)
    vmem = pl.BlockSpec(memory_space=pltpu.VMEM)

    def bf(*shape):
        return pltpu.VMEM(shape, BF)

    def fl(*shape):
        return pltpu.VMEM(shape, F32)

    def dma(*shape):
        return pltpu.SemaphoreType.DMA(shape)

    def x_first(n, rows, width):
        return [bf(n, 4, 2, rows, width), bf(n, 2, rows, width), bf(n, 2, 2, rows, width), bf(n, rows, width)]

    def z_first(n, rows, width):
        return [bf(n, 4, 2, rows, width), bf(n, 4, rows, width), bf(n, 2, rows // 2, width), bf(n, 2, rows, width)]

    scratch = [
        bf(8, 128, 1024), bf(NJ, 1024, 2 * CW), bf(NJ, 2, 512, CW), bf(NJ, 2, 512, CW), bf(NJ, 2, 512, CW),
        bf(4, 512, 512), bf(1024, 128), bf(128, NJ * CW),
        *x_first(NJ, 2 * XR, CW), *z_first(NJ, 2 * ZR, CW),
        *z_first(1, 128, 128),
        *x_first(NJ, 64, CW),
        bf(NJ, 2, 2, 128, CW), bf(8, 2, 2, 32, 128), bf(8, 2, 32, 128), bf(2, 256, 256),
        fl(2, 512, 128), bf(8, 128, 128), bf(8, 128, 128), bf(8, 128, 128), fl(128, 512), fl(128, 1024),
        dma(NJ, 6), dma(6), dma(11), dma(11), dma(24), dma(8, 2, 2),
        dma(NJ, 11), dma(NJ, 11), dma(NJ, 8), dma(NJ, 8), dma(1, 7), dma(1, 7),
        dma(NJ, 7), dma(NJ, 7),
        dma(NJ), dma(NJ), dma(8), dma(8), dma(8), dma(8), dma(8), dma(8),
    ]
    shapes = [((512, 1792), BF)] * 2 + [((128, 1792), BF)] + [((32, 1792), F32)] * 2 + [((64, 512), F32)] * 2
    held = pl.pallas_call(
        kernel,
        out_shape=tuple(pltpu.VMEM(shape, dtype) for shape, dtype in shapes),
        in_specs=[hbm] * 12,
        out_specs=(vmem,) * 7,
        scratch_shapes=scratch,
        compiler_params=pltpu.CompilerParams(
            collective_id=0, has_side_effects=True, vmem_limit_bytes=VMEM_LIMIT
        ),
        cost_estimate=pl.CostEstimate(flops=14_000_000_000, bytes_accessed=24_000_000, transcendentals=230_000),
    )(*args)
    outs = pl.pallas_call(
        write_out,
        out_shape=tuple(jax.ShapeDtypeStruct(shape, dtype) for shape, dtype in shapes),
        in_specs=[vmem] * 7,
        out_specs=(hbm,) * 7,
        scratch_shapes=[dma(13)],
        compiler_params=pltpu.CompilerParams(has_side_effects=True, vmem_limit_bytes=1024 * 1024),
    )(*held)
    return *outs[:5], outs[5].T, outs[6].T


def solution(mesh):
    rows, cols = P("dp", None), P(None, "col")
    both = P("dp", "col")
    return jax.shard_map(
        local,
        mesh=mesh,
        in_specs=(P("col", "dp"), both, both, rows, cols, rows, cols, rows, cols, rows, cols, both),
        out_specs=(both,) * 7,
        check_vma=False,
    )
```

```python
import jax
import jax.numpy as jnp
from jax import lax
from jax.experimental import pallas as pl
from jax.experimental.pallas import tpu as pltpu
from jax.sharding import PartitionSpec as P

adapter_scale = 0.5
MESH = pl.DeviceIdType.MESH
NJ = 7
CW = 256
UX = 16
XR, ZR = 64 + UX, 64 - UX
BF = jnp.bfloat16
F32 = jnp.float32
VMEM_LIMIT = 54 * 1024 * 1024


def f32(value):
    return value.astype(F32)


def dot(left, right, dims=((1,), (0,))):
    return lax.dot_general(left, right, (dims, ((), ())), preferred_element_type=F32)


def kernel(
    tokens, gate_w, up_w, gate_b_old, gate_a_old, up_b_old, up_a_old,
    gate_b_new, gate_right, up_b_new, up_right, hidden_grad,
    merged_gate, merged_up, hidden, gate_rg, up_rg, gate_lg, up_lg,
    tok, wts, raw, a_old, right, fac, low_w, hgrad,
    gp, gxo, gxn, gz, up, uz, uxo, uxn,
    lp, lz, lxo, lxn,
    rp, rxo, rxn, rz,
    delta, low_t, low_sib, low_sel,
    g_acc, g_send, g_recv, g_all, l_recv, l_send,
    in_sem, tok_in_sem, sib_s, sib_r, ag_s, ag_r,
    gp_s, gp_r, up_s, up_r, lp_s, lp_r, rp_s, rp_r,
    dl_s, dl_r, col_s, col_r, gcol_s, gcol_r, gdp_s, gdp_r,
):
    d = lax.axis_index("dp")
    c = lax.axis_index("col")
    q, k = d // 2, d % 2
    x, z = q // 2, q % 2
    zh, y = c // 4, c % 4
    xr, xl, xo = (x + 1) % 4, (x + 3) % 4, (x + 2) % 4
    yr, yl, yo = (y + 1) % 4, (y + 3) % 4, (y + 2) % 4

    def at_chip(xx, zz):
        return ((xx * 2 + zz) * 2 + k, c)

    def at_col(hh, yy):
        return (d, hh * 4 + yy)

    sibling = (q * 2 + 1 - k, c)
    to_right, to_left, to_z = at_chip(xr, z), at_chip(xl, z), at_chip(x, 1 - z)

    def remote(src, dst, send, recv, device):
        return pltpu.make_async_remote_copy(
            src_ref=src, dst_ref=dst, send_sem=send, recv_sem=recv,
            device_id=device, device_id_type=MESH,
        )

    weights = (gate_w, up_w, gate_a_old, up_a_old, gate_right, up_right)

    def load(n, j):
        held = (raw, raw, a_old, a_old, right, right)[n]
        cols = pl.ds(pl.multiple_of(j * CW, CW), CW)
        return pltpu.make_async_copy(weights[n].at[:, cols], held.at[j, n % 2], in_sem.at[j, n])

    factors = (gate_b_old, up_b_old, gate_b_new, up_b_new)

    def load_factor(n):
        return pltpu.make_async_copy(factors[n], fac.at[n], tok_in_sem.at[n])

    own_tokens = pltpu.make_async_copy(
        tokens.at[pl.ds(pl.multiple_of(k * 128, 128), 128)],
        tok.at[c, :, pl.ds(0, 512)], tok_in_sem.at[4],
    )
    load_hgrad = pltpu.make_async_copy(hidden_grad, hgrad, tok_in_sem.at[5])
    barrier = pltpu.get_barrier_semaphore()

    def greet(device):
        pl.semaphore_signal(barrier, inc=1, device_id=device, device_id_type=MESH)

    to_yr, to_yl, to_zo = at_col(zh, yr), at_col(zh, yl), at_col(1 - zh, y)
    greet(sibling)
    for there in (to_yr, to_yl, to_zo):
        greet((q * 2 + 1 - k, there[1]))
    for step in range(1, 8):
        greet((((q + step) % 8) * 2 + k, c))
        greet((d, (c + step) % 8))
    own_tokens.start()
    pl.semaphore_wait(barrier, 18)

    own, other = zh * 4, (1 - zh) * 4

    def rows_of(core, h):
        return tokens.at[pl.ds(pl.multiple_of(core * 128 + 64 * h, 64), 64)]

    def own_width(n, device, h, slot=c):
        dst = tok.at[slot, pl.ds(64 * h, 64), pl.ds(0, 512)]
        return remote(rows_of(k, h), dst, ag_s.at[12 * h + n], ag_r.at[slot, h, 0], device)

    def sib_width(n, device, h, slot=c):
        dst = tok.at[slot, pl.ds(64 * h, 64), pl.ds(512, 512)]
        there = (q * 2 + 1 - k, device[1])
        return remote(rows_of(1 - k, h), dst, ag_s.at[12 * h + n], ag_r.at[slot, h, 1], there)

    def block(n, slot, h, part, device):
        ref = tok.at[slot, pl.ds(64 * h, 64) if part is None else pl.ds(64 * h + 32 * part, 32)]
        return remote(ref, ref, ag_s.at[12 * h + n], ag_r.at[slot, h, part or 0], device)

    def direct(h):
        return (
            own_width(0, to_yr, h), own_width(1, to_yl, h), sib_width(2, to_yr, h), sib_width(3, to_yl, h),
            own_width(4, to_zo, h), sib_width(5, to_zo, h), sib_width(6, (d, c), h),
        )

    def passed(h):
        return (
            block(7, own + yl, h, 0, to_yr), block(8, own + yr, h, 1, to_yl),
            block(9, other + y, h, None, to_yr), block(10, other + y, h, None, to_yl),
            block(11, own + yo, h, None, to_zo),
        )

    def wait_direct(slot, h):
        own_width(0, to_yr, h, slot).wait_recv()
        sib_width(0, to_yr, h, slot).wait_recv()

    def pass_on(h):
        copies = passed(h)
        wait_direct(own + yl, h)
        copies[0].start()
        wait_direct(own + yr, h)
        copies[1].start()
        wait_direct(other + y, h)
        copies[2].start()
        copies[3].start()

    def pass_far(h):
        for part in range(2):
            block(0, own + yo, h, part, to_yr).wait_recv()
        passed(h)[4].start()

    def wait_rest(h):
        sib_width(0, to_yr, h).wait_recv()
        for slot in (other + yl, other + yr, other + yo):
            block(0, slot, h, None, to_yr).wait_recv()

    for copy in direct(0):
        copy.start()
    for n in range(4):
        load_factor(n).start()

    @pl.loop(0, NJ)
    def _(j):
        for n in range(6):
            load(n, j).start()

    load_hgrad.start()

    def send_weights(j):
        return remote(wts.at[j, pl.ds(0, 512)], wts.at[j, pl.ds(512, 512)], sib_s.at[2 + j], sib_r.at[2 + j], sibling)

    def merge(j):
        cols = pl.ds(pl.multiple_of(j * CW, CW), CW)
        for n in range(6):
            load(n, j).wait()
        for mat in range(2):
            merged = f32(raw[j, mat]) + adapter_scale * dot(fac[mat], a_old[j, mat])
            merged = merged.astype(BF)
            (merged_gate, merged_up)[mat][:, cols] = merged
            folded = f32(merged) + adapter_scale * dot(fac[2 + mat], right[j, mat])
            wts[j, 0:512, mat * CW:(mat + 1) * CW] = folded.astype(BF)
        send_weights(j).start()

    for n in range(4):
        load_factor(n).wait()
    low_cols = pl.ds(pl.multiple_of((c % 4) * 128, 128), 128)
    low_w[0:512, :] = jnp.where(c < 4, fac[2, :, low_cols], fac[3, :, low_cols])
    send_low_w = remote(low_w.at[pl.ds(0, 512)], low_w.at[pl.ds(512, 512)], sib_s.at[1], sib_r.at[1], sibling)
    send_low_w.start()

    class Sum:
        def parts(self, n):
            return (0, 1) if self.halves and n in self.first_copies else (None,)

        def copy(self, j, n, h=None):
            src, dst, device = self.pairs(j, slice(None) if h is None else pl.ds(self.half * h, self.half))[n]
            sem = n + 7 if h == 1 else n
            return remote(src, dst, self.send.at[j, sem], self.recv.at[j, sem], device)

        def step1(self, j, h=None):
            for n in self.first_copies:
                self.copy(j, n, h).start()

        def wait(self, j, n):
            for h in self.parts(n):
                self.copy(j, n, h).wait_recv()

        def drain(self, j):
            for n in range(7):
                for h in self.parts(n):
                    self.copy(j, n, h).wait_send()

    class XFirst(Sum):
        first_copies = (0, 1, 2, 3)

        def __init__(self, part, opp, near, last, send, recv, halves=False):
            self.part, self.opp, self.near, self.last = part, opp, near, last
            self.half = part.shape[3] // 2
            self.send, self.recv, self.halves = send, recv, halves

        def pairs(self, j, rows):
            part, opp, near = self.part, self.opp, self.near
            return (
                (part.at[j, xo, 0, rows], opp.at[j, 0, rows], to_right),
                (part.at[j, xo, 1, rows], opp.at[j, 1, rows], to_left),
                (part.at[j, xr, 1, rows], near.at[j, 0, 1, rows], to_right),
                (part.at[j, xl, 0, rows], near.at[j, 1, 0, rows], to_left),
                (part.at[j, xr, 0], near.at[j, 0, 0], to_right),
                (part.at[j, xl, 1], near.at[j, 1, 1], to_left),
                (part.at[j, x, 1 - z], self.last.at[j], to_z),
            )

        def step2(self, j):
            part = self.part
            self.wait(j, 0)
            part[j, xr, 0] = (f32(part[j, xr, 0]) + f32(self.opp[j, 0])).astype(BF)
            self.copy(j, 4).start()
            self.wait(j, 1)
            part[j, xl, 1] = (f32(part[j, xl, 1]) + f32(self.opp[j, 1])).astype(BF)
            self.copy(j, 5).start()

        def step3(self, j):
            for n in range(2, 6):
                self.wait(j, n)
            near = self.near
            self.part[j, x, 1 - z] = (
                f32(self.part[j, x, 1 - z]) + f32(near[j, 0, 1 - z]) + f32(near[j, 1, 1 - z])
            ).astype(BF)
            self.copy(j, 6).start()

        def final(self, j):
            self.wait(j, 6)
            near = self.near
            return f32(self.part[j, x, z]) + f32(near[j, 0, z]) + f32(near[j, 1, z]) + f32(self.last[j])

    class ZFirst(Sum):
        first_copies = (0,)

        def __init__(self, part, first, opp, near, send, recv, halves=False):
            self.part, self.first, self.opp, self.near = part, first, opp, near
            self.send, self.recv, self.halves = send, recv, halves
            self.half = self.rows = part.shape[3] // 2

        def pairs(self, j, rows):
            low, high = pl.ds(0, self.rows), pl.ds(self.rows, self.rows)
            part, opp, near = self.part, self.opp, self.near
            return (
                (part.at[j, :, 1 - z, rows], self.first.at[j, :, rows], to_z),
                (part.at[j, xo, z, low], opp.at[j, 0], to_right),
                (part.at[j, xo, z, high], opp.at[j, 1], to_left),
                (part.at[j, xr, z, high], near.at[j, 0, high], to_right),
                (part.at[j, xl, z, low], near.at[j, 1, low], to_left),
                (part.at[j, xr, z, low], near.at[j, 0, low], to_right),
                (part.at[j, xl, z, high], near.at[j, 1, high], to_left),
            )

        def step2(self, j):
            self.wait(j, 0)
            part = self.part
            for xx in (xo, xr, xl, x):
                part[j, xx, z] = (f32(part[j, xx, z]) + f32(self.first[j, xx])).astype(BF)
            for n in range(1, 5):
                self.copy(j, n).start()

        def step3(self, j):
            part, n = self.part, self.rows
            self.wait(j, 1)
            part[j, xr, z, 0:n] = (f32(part[j, xr, z, 0:n]) + f32(self.opp[j, 0])).astype(BF)
            self.copy(j, 5).start()
            self.wait(j, 2)
            part[j, xl, z, n:2 * n] = (f32(part[j, xl, z, n:2 * n]) + f32(self.opp[j, 1])).astype(BF)
            self.copy(j, 6).start()

        def final(self, j):
            for n in range(3, 7):
                self.wait(j, n)
            return f32(self.part[j, x, z]) + f32(self.near[j, 0]) + f32(self.near[j, 1])

    gate_sum = XFirst(gp, gxo, gxn, gz, gp_s, gp_r, halves=True)
    up_sum = ZFirst(up, uz, uxo, uxn, up_s, up_r, halves=True)
    low_sum = ZFirst(lp, lz, lxo, lxn, lp_s, lp_r)
    right_sum = XFirst(rp, rxo, rxn, rz, rp_s, rp_r)

    def low_copy(step):
        return remote(low_t.at[c], low_t.at[c], col_s.at[step], col_r.at[c], (d, (c + step) % 8))

    def low_wait(step):
        slot = (c + step) % 8
        remote(low_t.at[slot], low_t.at[slot], col_s.at[0], col_r.at[slot], sibling).wait_recv()

    send_low_sel = remote(low_t.at[:, :, 1 - k], low_sib, sib_s.at[9], sib_r.at[9], sibling)

    def low_start():
        for h in range(2):
            rows = tok[4 * h:4 * h + 4].reshape(512, 1024)
            lp[0, 2 * h:2 * h + 2] = dot(rows, low_w[...]).astype(BF).reshape(2, 2, 128, 128)
        low_sum.step1(0)

    def low_share():
        low_t[c] = low_sum.final(0).T.astype(BF).reshape(2, 2, 32, 128)
        for step in range(1, 8):
            low_copy(step).start()

    def low_swap():
        for step in range(1, 8):
            low_wait(step)
        send_low_sel.start()

    def low_pick():
        send_low_sel.wait_recv()
        for mat in range(2):
            low_sel[mat, :, 0:128] = low_t[4 * mat:4 * mat + 4, :, k].reshape(256, 128)
            low_sel[mat, :, 128:256] = low_sib[4 * mat:4 * mat + 4].reshape(256, 128)

    def products(j, h):
        part = slice(64 * h, 64 * h + 64)
        terms = dot(tok[:, part].reshape(512, 1024), wts[j]).astype(BF)
        terms = terms.reshape(4, 2, 64, 2 * CW)
        gp[j, :, :, XR * h:XR * h + 64] = terms[..., 0:CW]
        gp[j, :, :, XR * h + 64:XR * h + XR] = terms[:, :, 0:UX, CW:2 * CW]
        up[j, :, :, ZR * h:ZR * h + ZR] = terms[:, :, UX:64, CW:2 * CW]

    def rest_of_products(j):
        products(j, 1)
        gate_sum.step1(j, 1)
        up_sum.step1(j, 1)

        @pl.when(j > 2)
        def _():
            up_sum.step1(j, 0)

    def send_delta(j):
        return remote(delta.at[j, :, 0], delta.at[j, :, 1], dl_s.at[j], dl_r.at[j], sibling)

    def activate(j):
        cols = pl.ds(pl.multiple_of(j * CW, CW), CW)
        xs = gate_sum.final(j)
        zs = up_sum.final(j)
        gate = jnp.concatenate([xs[0:64], xs[XR:XR + 64]])
        upv = jnp.concatenate([xs[64:XR], zs[0:ZR], xs[XR + 64:2 * XR], zs[ZR:2 * ZR]])
        sg = 1.0 / (1.0 + jnp.exp(-gate))
        active = gate * sg
        hidden[:, cols] = (active * upv).astype(BF)
        upstream = f32(hgrad[:, cols])
        delta[j, 0, 0] = (upstream * upv * sg * (1.0 + gate * (1.0 - sg))).astype(BF)
        delta[j, 1, 0] = (upstream * active).astype(BF)
        send_delta(j).start()
        for mat in range(2):
            g_acc[mat] += dot(right[j, mat], delta[j, mat, 0], ((1,), (1,)))

    def right_products(j):
        send_delta(j).wait_recv()
        for mat in range(2):
            terms = dot(low_sel[mat], delta[j, mat].reshape(256, CW)).astype(BF)
            rp[j, :, :, 32 * mat:32 * mat + 32] = terms.reshape(4, 2, 32, CW)
        right_sum.step1(j)

    def right_final(j):
        cols = pl.ds(pl.multiple_of(j * CW, CW), CW)
        total = adapter_scale * right_sum.final(j)
        gate_rg[:, cols] = total[0:32]
        up_rg[:, cols] = total[32:64]

    def g_col(step):
        peer = (c + step) % 8
        return remote(g_send.at[peer], g_recv.at[c], gcol_s.at[step], gcol_r.at[c], (d, peer))

    def g_col_wait(step):
        slot = (c + step) % 8
        remote(g_send.at[slot], g_recv.at[slot], gcol_s.at[0], gcol_r.at[slot], sibling).wait_recv()

    def g_dp(step):
        return remote(g_all.at[q], g_all.at[q], gdp_s.at[step], gdp_r.at[q], (((q + step) % 8) * 2 + k, c))

    def g_dp_wait(step):
        slot = (q + step) % 8
        remote(g_all.at[slot], g_all.at[slot], gdp_s.at[0], gdp_r.at[slot], sibling).wait_recv()

    send_left = remote(l_send.at[:, pl.ds(512, 512)], l_recv, sib_s.at[10], sib_r.at[10], sibling)

    def g_start():
        for mat in range(2):
            g_send[:, 64 * mat:64 * mat + 64] = g_acc[mat].astype(BF).reshape(8, 64, 128)
        for step in range(1, 8):
            g_col(step).start()

    def g_share():
        total = f32(g_send[c])
        for step in range(1, 8):
            g_col_wait(step)
            total = total + f32(g_recv[(c + step) % 8])
        g_all[q] = total.astype(BF)
        for step in range(1, 8):
            g_dp(step).start()

    def left_products():
        for step in range(1, 8):
            g_dp_wait(step)
        g = jnp.concatenate([g_all[n] for n in range(8)], axis=1)
        l_send[:, 512:1024] = dot(g, tok[:, :, 512:1024].reshape(1024, 512))
        send_left.start()
        l_send[:, 0:512] = dot(g, tok[:, :, 0:512].reshape(1024, 512))

    def left_final():
        send_left.wait_recv()
        total = adapter_scale * (l_send[:, 0:512] + l_recv[...])
        gate_lg[...] = total[0:64]
        up_lg[...] = total[64:128]

    pass_on(0)
    for copy in direct(1):
        copy.start()
    pl.loop(0, 3)(merge)
    pass_far(0)
    pl.loop(3, NJ)(merge)
    own_tokens.wait()
    wait_rest(0)

    @pl.loop(0, 2)
    def _(j):
        send_weights(j).wait_recv()
        products(j, 0)
        gate_sum.step1(j, 0)
        up_sum.step1(j, 0)

    pass_on(1)

    @pl.loop(2, NJ)
    def _(j):
        send_weights(j).wait_recv()
        products(j, 0)
        gate_sum.step1(j, 0)

    pass_far(1)
    up_sum.step1(2, 0)
    send_low_w.wait_recv()
    wait_rest(1)
    load_hgrad.wait()
    g_acc[...] = jnp.zeros_like(g_acc)

    @pl.loop(0, NJ + 3)
    def _(i):
        def lag(n, *stages):
            @pl.when((i >= n) & (i < n + NJ))
            def _():
                for stage in stages:
                    stage(i - n)

        def once(n, stage):
            @pl.when(i == n)
            def _():
                stage()

        lag(0, rest_of_products)
        once(0, low_start)
        lag(1, gate_sum.step2, up_sum.step2)
        once(1, lambda: low_sum.step2(0))
        lag(2, gate_sum.step3, up_sum.step3)
        once(2, lambda: low_sum.step3(0))
        lag(3, activate)
        once(NJ + 2, g_start)
        once(3, low_share)
        once(4, low_swap)
        once(5, low_pick)
        lag(5, right_products)
        lag(6, right_sum.step2)
        lag(7, right_sum.step3)
        lag(8, right_final)

    @pl.loop(NJ - 2, NJ)
    def _(j):
        right_products(j)

    right_sum.step2(NJ - 3)
    g_share()

    @pl.loop(NJ - 2, NJ)
    def _(j):
        right_sum.step2(j)
        right_sum.step3(j - 2)
        right_final(j - 3)

    right_sum.step3(NJ - 2)
    right_sum.step3(NJ - 1)
    left_products()

    @pl.loop(NJ - 3, NJ)
    def _(j):
        right_final(j)

    left_final()

    @pl.loop(0, NJ)
    def _(j):
        for total in (gate_sum, up_sum, right_sum):
            total.drain(j)
        send_weights(j).wait_send()
        send_delta(j).wait_send()

    low_sum.drain(0)
    send_low_w.wait_send()
    send_low_sel.wait_send()
    send_left.wait_send()
    for h in range(2):
        for copy in direct(h) + passed(h):
            copy.wait_send()
    for step in range(1, 8):
        low_copy(step).wait_send()
        g_col(step).wait_send()
        g_dp(step).wait_send()


def write_out(*refs):
    sems = refs[-1]
    pieces = [(n, pl.ds(128 * m, 128)) for n in range(2) for m in range(4)] + [(n, slice(None)) for n in range(2, 7)]
    copies = [
        pltpu.make_async_copy(refs[n].at[rows], refs[7 + n].at[rows], sems.at[m])
        for m, (n, rows) in enumerate(pieces)
    ]
    for copy in copies:
        copy.start()
    for copy in copies:
        copy.wait()


def local(*args):
    hbm = pl.BlockSpec(memory_space=pl.ANY)
    vmem = pl.BlockSpec(memory_space=pltpu.VMEM)

    def bf(*shape):
        return pltpu.VMEM(shape, BF)

    def fl(*shape):
        return pltpu.VMEM(shape, F32)

    def dma(*shape):
        return pltpu.SemaphoreType.DMA(shape)

    def x_first(n, rows, width):
        return [bf(n, 4, 2, rows, width), bf(n, 2, rows, width), bf(n, 2, 2, rows, width), bf(n, rows, width)]

    def z_first(n, rows, width):
        return [bf(n, 4, 2, rows, width), bf(n, 4, rows, width), bf(n, 2, rows // 2, width), bf(n, 2, rows, width)]

    scratch = [
        bf(8, 128, 1024), bf(NJ, 1024, 2 * CW), bf(NJ, 2, 512, CW), bf(NJ, 2, 512, CW), bf(NJ, 2, 512, CW),
        bf(4, 512, 512), bf(1024, 128), bf(128, NJ * CW),
        *x_first(NJ, 2 * XR, CW), *z_first(NJ, 2 * ZR, CW),
        *z_first(1, 128, 128),
        *x_first(NJ, 64, CW),
        bf(NJ, 2, 2, 128, CW), bf(8, 2, 2, 32, 128), bf(8, 2, 32, 128), bf(2, 256, 256),
        fl(2, 512, 128), bf(8, 128, 128), bf(8, 128, 128), bf(8, 128, 128), fl(128, 512), fl(128, 1024),
        dma(NJ, 6), dma(6), dma(11), dma(11), dma(24), dma(8, 2, 2),
        dma(NJ, 11), dma(NJ, 11), dma(NJ, 8), dma(NJ, 8), dma(1, 7), dma(1, 7),
        dma(NJ, 7), dma(NJ, 7),
        dma(NJ), dma(NJ), dma(8), dma(8), dma(8), dma(8), dma(8), dma(8),
    ]
    shapes = [((512, 1792), BF)] * 2 + [((128, 1792), BF)] + [((32, 1792), F32)] * 2 + [((64, 512), F32)] * 2
    held = pl.pallas_call(
        kernel,
        out_shape=tuple(pltpu.VMEM(shape, dtype) for shape, dtype in shapes),
        in_specs=[hbm] * 12,
        out_specs=(vmem,) * 7,
        scratch_shapes=scratch,
        compiler_params=pltpu.CompilerParams(
            collective_id=0, has_side_effects=True, vmem_limit_bytes=VMEM_LIMIT
        ),
        cost_estimate=pl.CostEstimate(flops=14_000_000_000, bytes_accessed=24_000_000, transcendentals=230_000),
    )(*args)
    outs = pl.pallas_call(
        write_out,
        out_shape=tuple(jax.ShapeDtypeStruct(shape, dtype) for shape, dtype in shapes),
        in_specs=[vmem] * 7,
        out_specs=(hbm,) * 7,
        scratch_shapes=[dma(13)],
        compiler_params=pltpu.CompilerParams(has_side_effects=True, vmem_limit_bytes=1024 * 1024),
    )(*held)
    return *outs[:5], outs[5].T, outs[6].T


def solution(mesh):
    rows, cols = P("dp", None), P(None, "col")
    both = P("dp", "col")
    return jax.shard_map(
        local,
        mesh=mesh,
        in_specs=(P("col", "dp"), both, both, rows, cols, rows, cols, rows, cols, rows, cols, both),
        out_specs=(both,) * 7,
        check_vma=False,
    )
```
